128 devices in a mesh: row: 8 (over z_lo, x), col: 16 (over z_hi, y, core).
Axes of the slice: x: 4, y: 4, z: 4 (z_hi: 2, z_lo: 2; z = z_hi * 2 + z_lo), core: 2. Of those that a mesh axis runs over, the one named last changes fastest.
Arguments:
- trial: float32 [524288], P(('row', 'col')), may hold values from -6 to 6
- energies: float32 [524288], P(('row', 'col')), may hold values from 0.5 to 3
- densities: bfloat16 [8192, 64, 512], P(('row', 'col')), may hold values from -0.75 to 0.75
- screening: bfloat16 [1048576, 512], P(('row', 'col')), may hold values from 0.0099487305 to 0.099609375
- pair_index: int32 [2, 1048576], P(None, ('row', 'col')), may hold values from 0 to 8191, as said below
- pair_count: int32 [128], P(('row', 'col')), may hold values from 1024 to 8192, as said below
- recycled: float32 [20, 524288], P(None, ('row', 'col'))
Outputs:
- image: float32 [524288], P(('row', 'col'))
- coefficients: float32 [20], replicated
The draws below stay inside these ranges and needn't reach their ends.
Inputs may be any that keep to these rules, and one draw needn't show every extreme that they name: `pair_index`: slot p of device d = p // 8192 (devices numbered row-major over row and col) holds rows[p] among the k-points of the devices in d's row index and cols[p] among those of the devices in d's col index. `pair_count`: one device is full in every draw.
All inputs are finite; a program needn't handle non-finite values.
Results may differ from the reference program's by a relative error of at most 0.014.
Values may be sent and summed in bfloat16 or wider, within the bound.
No kernel may reach another device: no remote copies, remote signals or barrier semaphores. Data moves between devices by JAX's collectives and lax.ppermute only.
A program may use at most 192 MiB of HBM per device.

```python
import math
import jax
import jax.numpy as jnp
from jax import lax

NT = 64
NG = 512
NRV = 20
KD = 64
P_DEV = 8192
NK = 8192
N_ROW = 8
N_COL = 16
DEVICES = 128


def draw_pair_index(key, part):
    key = jax.random.fold_in(key, 11)
    first_key, second_key = jax.random.split(key)
    total_slots = DEVICES * P_DEV
    owner = jnp.arange(total_slots) // P_DEV
    owner_row = owner // N_COL
    owner_col = owner % N_COL
    row_offset = jax.random.randint(first_key, (total_slots,), 0, N_COL * KD)
    col_offset = jax.random.randint(second_key, (total_slots,), 0, N_ROW * KD)
    row_global = owner_row * N_COL * KD + row_offset
    col_global = (col_offset // KD * N_COL + owner_col) * KD + col_offset % KD
    return jnp.stack([row_global, col_global]).astype(jnp.int32)


def draw_pair_count(key, part):
    key = jax.random.fold_in(key, 23)
    first_key, second_key = jax.random.split(key)
    base_count = P_DEV // 8 + jax.random.randint(first_key, (DEVICES,), 0, P_DEV // 2)
    fullest = jax.random.randint(second_key, (), 0, DEVICES)
    return jnp.where(jnp.arange(DEVICES) == fullest, P_DEV, base_count).astype(jnp.int32)


def draw_recycled(key, part):
    key = jax.random.fold_in(key, 37)
    position = (jnp.arange(NK * NT) // NT).astype(jnp.float32) / NK
    values = jax.random.normal(key, (NRV, NK * NT), jnp.float32) * 3.0 ** position
    return (values * 2.0 / jnp.sqrt(float(NK * NT))).astype(jnp.float32)


def block_scale(own_key, shape, shards, least, top_value):
    gain = 1.0
    for axis_at, blocks in shards:
        heights = jax.random.uniform(jax.random.fold_in(jax.random.fold_in(own_key, 6), axis_at), (blocks,), jnp.float32, least / len(shards), top_value / len(shards))
        gain = gain * jnp.repeat(jnp.exp(heights), shape[axis_at] // blocks).reshape((-1,) + (1,) * (len(shape) - 1 - axis_at))
    return gain


def noise(own_key, shape, spread, most, pieces=(), kind=jnp.bfloat16):
    loudness = block_scale(own_key, shape, pieces, -0.22, 0.18) if pieces else 1.0
    array = jax.random.normal(own_key, shape, jnp.float32) * spread * loudness
    return jnp.minimum(jnp.maximum(array, -most), most).astype(kind)


def setup_inputs(seed: int = 0) -> dict:
    key_of = jax.random.split(jax.random.key(seed), 8)
    return {
        "trial": noise(key_of[0], (NK * NT,), 1.0, 6.0, ((0, 128),), jnp.float32),
        "energies": jnp.clip(jnp.exp(math.log(3.0) - 1.7917595 * jax.random.uniform(key_of[1], (NK * NT,), jnp.float32) ** block_scale(key_of[1], (NK * NT,), ((0, 128),), -0.2, 0.2)), 0.5, 3.0),
        "densities": noise(key_of[2], (NK, NT, NG), NT ** -0.5, 0.75, ((0, 128),)),
        "screening": jnp.clip(jnp.exp(math.log(0.099609375) - 2.3038113 * jax.random.uniform(key_of[3], (DEVICES * P_DEV, NG), jnp.float32) ** block_scale(key_of[3], (DEVICES * P_DEV, NG), ((0, 128),), -0.2, 0.2)), 0.0099487305, 0.099609375).astype(jnp.bfloat16),
        "pair_index": draw_pair_index(jax.random.fold_in(key_of[7], 71), 0),
        "pair_count": draw_pair_count(jax.random.fold_in(key_of[7], 71), 0),
        "recycled": draw_recycled(jax.random.fold_in(key_of[7], 71), 0),
    }


def add_terms(totals, table, source_index, target_index, weights):
    picked = jnp.take(table, source_index, axis=0).astype(jnp.float32)
    slot_terms = (weights * picked).astype(jnp.bfloat16)
    slot_terms = lax.optimization_barrier(slot_terms)
    return totals.at[target_index].add(slot_terms.astype(jnp.float32))


def rounded(values):
    return lax.optimization_barrier(values.astype(jnp.bfloat16)).astype(jnp.float32)


def reference(trial, energies, densities, screening, pair_index, pair_count, recycled):
    groups = NK // KD
    trial_b = lax.optimization_barrier(trial.astype(jnp.bfloat16)).astype(jnp.float32)
    dens_groups = densities.reshape(groups, KD, NT, NG)

    def project(item):
        trial_group, dens_group = item
        return jnp.einsum("kt,ktg->kg", trial_group, dens_group.astype(jnp.float32))

    pair_dens = lax.map(project, (trial_b.reshape(groups, KD, NT), dens_groups))
    pair_dens = pair_dens.reshape(NK, NG).astype(jnp.bfloat16)

    def device_step(totals, item):
        weights, row_index, col_index, live_count = item
        live_slots = jnp.arange(P_DEV) < live_count
        weights = jnp.where(live_slots[:, None], weights.astype(jnp.float32), 0.0)
        empty = jnp.zeros((NK, NG), jnp.float32)
        row_part = add_terms(empty, pair_dens, col_index, row_index, weights)
        col_part = add_terms(empty, pair_dens, row_index, col_index, weights)
        totals = totals + rounded(row_part) + rounded(col_part)
        return totals, None

    items = (screening.reshape(DEVICES, P_DEV, NG),
             pair_index[0].reshape(DEVICES, P_DEV).astype(jnp.int32),
             pair_index[1].reshape(DEVICES, P_DEV).astype(jnp.int32),
             pair_count)
    totals, unused = lax.scan(device_step, jnp.zeros((NK, NG), jnp.float32), items)
    field_b = rounded(totals)

    def expand(item):
        field_group, dens_group = item
        return jnp.einsum("kg,ktg->kt", field_group, dens_group.astype(jnp.float32))

    kernel_part = lax.map(expand, (field_b.reshape(groups, KD, NG), dens_groups)).reshape(NK * NT)
    product = energies * trial + kernel_part
    coefficients = jnp.dot(recycled, product, precision=lax.Precision.HIGHEST)
    image = product - jnp.dot(coefficients, recycled, precision=lax.Precision.HIGHEST)
    return image, coefficients
```

```python
import functools

import jax
import jax.numpy as jnp
from jax import lax
from jax.experimental import pallas as pl
from jax.experimental.pallas import tpu as pltpu
from jax.sharding import Mesh, PartitionSpec as P

AXES = ("zl", "x", "zh", "y", "c")
F32 = jnp.float32
BF16 = jnp.bfloat16
CHUNK = 512
COPIES = 4
UNROLL = 4


def slot_kernel(rows, cols, count, weights, own_dens, other_dens, col_dens,
                own_total, other_total, col_total, weight_buf, spread, *rest):
    row_tables, col_tables, sem = rest[:COPIES], rest[COPIES:2 * COPIES], rest[2 * COPIES]
    live = count[0]
    chunks = (live + CHUNK - 1) // CHUNK

    def copy(i):
        part = pl.ds(i * CHUNK, CHUNK)
        return pltpu.make_async_copy(weights.at[part], weight_buf.at[part], sem.at[i])

    def start(i, _):
        copy(i).start()
        return 0

    lax.fori_loop(0, chunks, start, 0)
    zeros = jnp.zeros((4, 128), F32)

    def fill(source, tables, first, dens_first):
        def step(i, _):
            part = source[pl.ds(pl.multiple_of(i * 16, 16), 16), :].astype(F32)
            for t in range(4):
                dens = part[4 * t:4 * t + 4]
                entry = jnp.concatenate([dens, zeros] if dens_first else [zeros, dens], 0)
                for table in tables:
                    table[pl.ds(pl.multiple_of((first + i * 4 + t) * 8, 8), 8), :] = entry
            return 0

        lax.fori_loop(0, source.shape[0] // 16, step, 0, unroll=2)

    half = own_dens.shape[0] // 4
    fill(own_dens, row_tables, 0, True)
    fill(other_dens, row_tables, half, True)
    fill(col_dens, col_tables, 0, False)

    def one(slot, group, lane, which):
        low = lax.broadcasted_iota(jnp.int32, (8, 128), 0) >= 4
        w = spread[pl.ds(group * 64 + lane, 8, stride=8), :]
        r = pl.ds(pl.multiple_of(rows[slot], 8), 8)
        c = pl.ds(pl.multiple_of(cols[slot], 8), 8)
        row_entry = row_tables[which][r, :]
        col_entry = col_tables[which][c, :]
        row_tables[which][r, :] = row_entry + jnp.where(low, w, 0.0) * col_entry
        col_tables[which][c, :] = col_entry + jnp.where(low, 0.0, w) * row_entry

    def chunk(i, _):
        copy(i).wait()
        left = jnp.minimum(live - i * CHUNK, CHUNK)

        def relayout(g, _):
            v = weight_buf[pl.ds(pl.multiple_of(i * CHUNK + g * 16, 16), 16), :].astype(F32)
            for h in range(2):
                for j in range(4):
                    tile = v[8 * h:8 * h + 8, 128 * j:128 * j + 128]
                    for twice in range(2):
                        at = g * 128 + h * 64 + twice * 32 + j * 8
                        spread[pl.ds(pl.multiple_of(at, 8), 8), :] = tile
            return 0

        lax.fori_loop(0, CHUNK // 16, relayout, 0, unroll=2)
        wide = left // (8 * UNROLL)

        def groups(g, _):
            for t in range(UNROLL):
                for u in range(8):
                    group = g * UNROLL + t
                    one(i * CHUNK + group * 8 + u, group, u, u % COPIES)
            return 0

        lax.fori_loop(0, wide, groups, 0)

        def tail(t, _):
            slot = wide * 8 * UNROLL + t
            one(i * CHUNK + slot, slot // 8, slot % 8, 0)
            return 0

        lax.fori_loop(0, left - wide * 8 * UNROLL, tail, 0)
        return 0

    lax.fori_loop(0, chunks, chunk, 0)

    def drain(tables, first, target, at):
        def step(i, _):
            parts = []
            for t in range(4):
                entry = pl.ds(pl.multiple_of((first + i * 4 + t) * 8, 8), 8)
                total = tables[0][entry, :]
                for table in tables[1:]:
                    total = total + table[entry, :]
                parts.append(total[at:at + 4])
            rows16 = pl.ds(pl.multiple_of(i * 16, 16), 16)
            target[rows16, :] = jnp.concatenate(parts, 0).astype(BF16)
            return 0

        lax.fori_loop(0, target.shape[0] // 16, step, 0, unroll=4)

    drain(row_tables, 0, own_total, 4)
    drain(row_tables, half, other_total, 4)
    drain(col_tables, 0, col_total, 0)


def pair_terms(rows, cols, count, weights, own_dens, other_dens, col_dens):
    smem = pl.BlockSpec(memory_space=pltpu.SMEM)
    vmem = pl.BlockSpec(memory_space=pltpu.VMEM)
    outs = [jax.ShapeDtypeStruct(a.shape, BF16) for a in (own_dens, other_dens, col_dens)]
    row_table = pltpu.VMEM((4 * own_dens.shape[0], 128), F32)
    col_table = pltpu.VMEM((2 * col_dens.shape[0], 128), F32)
    return pl.pallas_call(
        slot_kernel,
        out_shape=outs,
        in_specs=[smem, smem, smem, pl.BlockSpec(memory_space=pl.ANY), vmem, vmem, vmem],
        out_specs=[vmem, vmem, vmem],
        scratch_shapes=[
            pltpu.VMEM(weights.shape, BF16),
            pltpu.VMEM((CHUNK * 8, 128), F32),
            *[row_table] * COPIES,
            *[col_table] * COPIES,
            pltpu.SemaphoreType.DMA((weights.shape[0] // CHUNK,)),
        ],
        compiler_params=pltpu.CompilerParams(vmem_limit_bytes=56 * 2**20),
    )(rows, cols, count, weights, own_dens, other_dens, col_dens)


def body(trial, energies, densities, screening, pair_index, pair_count, recycled):
    kpoints, transitions, gvectors = densities.shape
    lanes = 128
    per_k = gvectors // lanes
    col_devices = lax.axis_size("zh") * lax.axis_size("y") * lax.axis_size("c")
    chips = lax.axis_size("zh") * lax.axis_size("y")
    row_place = lax.axis_index("zl") * lax.axis_size("x") + lax.axis_index("x")
    core = lax.axis_index("c")
    swap = [(0, 1), (1, 0)]

    row_local = pair_index[0] - row_place * col_devices * kpoints
    owner = row_local // kpoints
    rows = (((owner % 2) ^ core) * chips + owner // 2) * kpoints + row_local % kpoints
    cols = pair_index[1] // (col_devices * kpoints) * kpoints + pair_index[1] % kpoints

    trial_b = trial.reshape(kpoints, transitions).astype(BF16)
    local_dens = jnp.einsum(
        "kt,ktg->kg", trial_b, densities, preferred_element_type=F32
    ).astype(BF16).reshape(kpoints * per_k, lanes)

    def gather(values, axes):
        size = 1
        for a in axes:
            size *= lax.axis_size(a)
        spread = jnp.broadcast_to(values[None], (size,) + values.shape)
        return lax.all_to_all(spread, axes, 0, 0).reshape(-1, lanes)

    own_dens = gather(local_dens, ("zh", "y"))
    other_dens = lax.ppermute(own_dens, "c", swap)
    col_dens = gather(local_dens, ("zl", "x"))

    own_total, other_total, col_total = pair_terms(
        rows * 8, cols * 8, pair_count, screening, own_dens, other_dens, col_dens)

    def scatter(values, axes):
        parts = values.reshape(-1, kpoints * per_k, lanes)
        return jnp.sum(lax.all_to_all(parts, axes, 0, 0).astype(F32), 0)

    from_other = lax.ppermute(other_total, "c", swap)
    row_total = (own_total.astype(F32) + from_other.astype(F32)).astype(BF16)
    field = scatter(col_total, ("zl", "x")) + scatter(row_total, ("zh", "y"))
    field_b = field.astype(BF16).reshape(kpoints, gvectors)
    kernel_part = jnp.einsum("kg,ktg->kt", field_b, densities, preferred_element_type=F32)
    product = energies * trial + kernel_part.reshape(kpoints * transitions)
    local_proj = jnp.dot(recycled, product, precision=lax.Precision.HIGHEST)
    devices = col_devices * lax.axis_size("zl") * lax.axis_size("x")
    spread = jnp.broadcast_to(local_proj[None], (devices,) + local_proj.shape)
    coefficients = jnp.sum(lax.all_to_all(spread, AXES, 0, 0, tiled=True), 0)
    image = product - jnp.dot(coefficients, recycled, precision=lax.Precision.HIGHEST)
    return (image, coefficients)


def solution(mesh):
    fine = Mesh(mesh.devices.reshape(2, 4, 2, 4, 2), AXES)
    placed = (
        P(AXES),
        P(AXES),
        P(AXES, None, None),
        P(AXES, None),
        P(None, AXES),
        P(AXES),
        P(None, AXES),
    )
    return jax.shard_map(
        body, mesh=fine, in_specs=placed, out_specs=(P(AXES), P()), check_vma=False
    )
```

```python
import functools

import jax
import jax.numpy as jnp
import numpy as np
from jax import lax
from jax.experimental import pallas as pl
from jax.experimental.pallas import tpu as pltpu
from jax.sharding import Mesh, PartitionSpec as P

AXES = ("zl", "x", "zh", "y", "c")
F32 = jnp.float32
BF16 = jnp.bfloat16
CHUNK = 512
COPIES = 4
SLOT_MIB = 40
SMALL_MIB = 6
UNROLL = 4


def slot_kernel(rows, cols, count, place, weights, mine, theirs, keep, send, spread, *rest):
    row_tables, col_tables = rest[:COPIES], rest[COPIES:]
    live, core = count[0], place[0]
    chunks = (live + CHUNK - 1) // CHUNK
    zeros = jnp.zeros((4, 128), F32)

    half = mine.shape[0] // 2
    block = half // (mine.shape[0] // 512)

    def fill(source, tables, count, dens_first, at):
        def step(i, _):
            part = source[pl.ds(pl.multiple_of(at(i), 16), 16), :].astype(F32)
            for t in range(4):
                dens = part[4 * t:4 * t + 4]
                entry = jnp.concatenate([dens, zeros] if dens_first else [zeros, dens], 0)
                for table in tables:
                    table[pl.ds(pl.multiple_of((i * 4 + t) * 8, 8), 8), :] = entry
            return 0

        lax.fori_loop(0, count // 16, step, 0, unroll=4)

    def whole(i):
        return i * 16

    def one_core(which):
        per = block // 16
        return lambda i: (i // per) * (2 * block) + which * block + (i % per) * 16

    @pl.when(core == 0)
    def _():
        fill(mine, row_tables, 2 * half, True, whole)
        fill(theirs, col_tables, half, False, one_core(0))

    @pl.when(core != 0)
    def _():
        fill(theirs, row_tables, 2 * half, True, whole)
        fill(mine, col_tables, half, False, one_core(1))

    low = lax.broadcasted_iota(jnp.int32, (8, 128), 0) >= 4

    def one(slot, which, row_weight, col_weight):
        r = pl.ds(pl.multiple_of(rows[slot], 8), 8)
        c = pl.ds(pl.multiple_of(cols[slot], 8), 8)
        row_entry = row_tables[which][r, :]
        col_entry = col_tables[which][c, :]
        row_tables[which][r, :] = row_entry + row_weight * col_entry
        col_tables[which][c, :] = col_entry + col_weight * row_entry

    def chunk(i, _):
        left = jnp.minimum(live - i * CHUNK, CHUNK)

        def relayout(g, _):
            v = weights[pl.ds(pl.multiple_of(i * CHUNK + g * 16, 16), 16), :].astype(F32)
            for h in range(2):
                for j in range(4):
                    at = pl.ds(pl.multiple_of(g * 64 + h * 32 + j * 8, 8), 8)
                    spread[at, :] = v[8 * h:8 * h + 8, 128 * j:128 * j + 128]
            return 0

        lax.fori_loop(0, CHUNK // 16, relayout, 0, unroll=4)
        wide = left // (16 * UNROLL)

        def groups(g, _):
            for t in range(UNROLL):
                for u in range(8):
                    group = g * UNROLL + t
                    slot = i * CHUNK + group * 16 + u
                    both = spread[pl.ds(group * 64 + u, 8, stride=8), :]
                    turned = jnp.concatenate([both[4:8], both[0:4]], 0)
                    one(slot, (2 * u) % COPIES, jnp.where(low, turned, 0.0), jnp.where(low, 0.0, both))
                    one(slot + 8, (2 * u + 1) % COPIES, jnp.where(low, both, 0.0), jnp.where(low, 0.0, turned))
            return 0

        lax.fori_loop(0, wide, groups, 0)

        def tail(t, _):
            slot = wide * 16 * UNROLL + t
            w = spread[pl.ds(slot // 8 * 32 + slot % 8, 4, stride=8), :]
            w = jnp.concatenate([w, w], 0)
            one(i * CHUNK + slot, 0, jnp.where(low, w, 0.0), jnp.where(low, 0.0, w))
            return 0

        lax.fori_loop(0, left - wide * 16 * UNROLL, tail, 0)
        return 0

    lax.fori_loop(0, chunks, chunk, 0)

    def drain(tables, target, count, at, offset):
        def step(i, _):
            parts = []
            for t in range(4):
                entry = pl.ds(pl.multiple_of((i * 4 + t) * 8, 8), 8)
                total = tables[0][entry, :]
                for table in tables[1:]:
                    total = total + table[entry, :]
                parts.append(total[offset:offset + 4])
            rows16 = pl.ds(pl.multiple_of(at(i), 16), 16)
            target[rows16, :] = jnp.concatenate(parts, 0).astype(BF16)
            return 0

        lax.fori_loop(0, count // 16, step, 0, unroll=8)

    def clear(target, at):
        def step(i, _):
            target[pl.ds(pl.multiple_of(at(i), 16), 16), :] = jnp.zeros((16, 128), BF16)
            return 0

        lax.fori_loop(0, half // 16, step, 0, unroll=8)

    @pl.when(core == 0)
    def _():
        drain(row_tables, keep, 2 * half, whole, 4)
        drain(col_tables, send, half, one_core(0), 0)
        clear(send, one_core(1))

    @pl.when(core != 0)
    def _():
        drain(row_tables, send, 2 * half, whole, 4)
        drain(col_tables, keep, half, one_core(1), 0)
        clear(keep, one_core(0))


def pair_terms(rows, cols, count, place, weights, mine, theirs):
    smem = pl.BlockSpec(memory_space=pltpu.SMEM)
    vmem = pl.BlockSpec(memory_space=pltpu.VMEM)
    row_table = pltpu.VMEM((2 * mine.shape[0], 128), F32)
    col_table = pltpu.VMEM((mine.shape[0], 128), F32)
    return pl.pallas_call(
        slot_kernel,
        out_shape=[jax.ShapeDtypeStruct(mine.shape, BF16)] * 2,
        in_specs=[smem] * 4 + [vmem] * 3,
        out_specs=[vmem, vmem],
        scratch_shapes=[
            pltpu.VMEM((CHUNK * 4, 128), F32), *[row_table] * COPIES, *[col_table] * COPIES],
        compiler_params=pltpu.CompilerParams(vmem_limit_bytes=SLOT_MIB * 2**20),
    )(rows, cols, count, place, weights, mine, theirs)


def local_call(kernel, outs, *args, scalars=0, flops=0):
    smem = pl.BlockSpec(memory_space=pltpu.SMEM)
    vmem = pl.BlockSpec(memory_space=pltpu.VMEM)
    return pl.pallas_call(
        kernel,
        out_shape=outs,
        in_specs=[smem] * scalars + [vmem] * (len(args) - scalars),
        out_specs=jax.tree.map(lambda _: vmem, outs),
        cost_estimate=pl.CostEstimate(flops=flops, bytes_accessed=0, transcendentals=0) if flops else None,
        compiler_params=pltpu.CompilerParams(vmem_limit_bytes=SMALL_MIB * 2**20),
    )(*args)


def pack_kernel(kpoints, spans, place, first_row, local, other, pair_index, out, rows, cols):
    index = pair_index[...]
    rows[...] = ((index[0:1, :] - first_row[0]) * 8).reshape(rows.shape)
    col = index[1:2, :]
    cols[...] = ((col // spans * kpoints + col % kpoints) * 8).reshape(cols.shape)
    size = local.shape[0]

    def step(i, _):
        at = pl.ds(pl.multiple_of(i * 16, 16), 16)
        first, second = local[at, :], other[at, :]
        swapped = place[0] != 0
        low = jnp.where(swapped, second.astype(F32), first.astype(F32)).astype(BF16)
        high = jnp.where(swapped, first.astype(F32), second.astype(F32)).astype(BF16)
        for n in range(out.shape[0]):
            out[n, at, :] = low
            out[n, pl.ds(pl.multiple_of(size + i * 16, 16), 16), :] = high
        return 0

    lax.fori_loop(0, size // 16, step, 0, unroll=2)


def add_kernel(keep, got, out):
    def step(i, _):
        at = pl.ds(pl.multiple_of(i * 16, 16), 16)
        out[at, :] = (keep[at, :].astype(F32) + got[at, :].astype(F32)).astype(BF16)
        return 0

    lax.fori_loop(0, keep.shape[0] // 16, step, 0, unroll=8)


def sum_kernel(place, parts, here, there):
    size = here.shape[0]

    def step(i, _):
        at = pl.ds(pl.multiple_of(i * 16, 16), 16)
        for target, which in ((here, place[0]), (there, 1 - place[0])):
            first = pl.ds(pl.multiple_of(which * size + i * 16, 16), 16)
            total = parts[0, first, :].astype(F32)
            for n in range(1, parts.shape[0]):
                total = total + parts[n, first, :].astype(F32)
            target[at, :] = total
        return 0

    lax.fori_loop(0, size // 16, step, 0, unroll=4)


def project_kernel(trial, densities, out, wide):
    kpoints = out.shape[0] // 4
    span = densities.shape[0] * 8 // kpoints
    rows8 = lax.broadcasted_iota(jnp.int32, (8, span), 0)
    owner = lax.broadcasted_iota(jnp.int32, (8, span), 1) // (span // 8)
    for g in range(kpoints // 8):
        line = jnp.broadcast_to(trial[g * span:(g + 1) * span].reshape(1, span), (8, span))
        left = jnp.where(rows8 == owner, line, 0.0).astype(BF16)
        dens = jnp.dot(left, densities[g * span:(g + 1) * span, :], preferred_element_type=F32)
        for j in range(4):
            wide[pl.ds(32 * g + j, 8, stride=4), :] = dens[:, 128 * j:128 * j + 128]
    out[...] = wide[...].astype(BF16)


def project(trial, densities):
    kpoints, transitions, gvectors = densities.shape
    vmem = pl.BlockSpec(memory_space=pltpu.VMEM)
    return pl.pallas_call(
        project_kernel,
        out_shape=jax.ShapeDtypeStruct((kpoints * 4, 128), BF16),
        in_specs=[vmem, vmem],
        out_specs=vmem,
        scratch_shapes=[pltpu.VMEM((kpoints * 4, 128), F32)],
        cost_estimate=pl.CostEstimate(flops=4 * 10**9, bytes_accessed=0, transcendentals=0),
        compiler_params=pltpu.CompilerParams(vmem_limit_bytes=SMALL_MIB * 2**20),
    )(trial, densities.reshape(-1, gvectors))


def expand_kernel(here, there, densities, trial, energies, recycled, product, projections):
    kpoints = here.shape[0] // 4
    span = densities.shape[0] * 8 // kpoints
    rows8 = lax.broadcasted_iota(jnp.int32, (8, span), 0)
    owner = lax.broadcasted_iota(jnp.int32, (8, span), 1) // (span // 8)
    sums = jnp.zeros((recycled.shape[0], 128), F32)
    for g in range(kpoints // 8):
        field = []
        for j in range(4):
            at = pl.ds(32 * g + j, 8, stride=4)
            field.append(here[at, :] + there[at, :])
        every = lax.dot_general(
            jnp.concatenate(field, 1).astype(BF16), densities[g * span:(g + 1) * span, :],
            (((1,), (1,)), ((), ())), preferred_element_type=F32)
        part = jnp.sum(jnp.where(rows8 == owner, every, 0.0), 0, keepdims=True)
        at = pl.ds(g * span, span)
        line = (energies[at] * trial[at]).reshape(1, span) + part
        product[at] = line.reshape(span)
        weighted = recycled[:, g * span:(g + 1) * span] * line
        for j in range(span // 128):
            sums = sums + weighted[:, 128 * j:128 * j + 128]
    total = jnp.sum(sums, 1, keepdims=True)
    count = total.shape[0]
    at = lax.broadcasted_iota(jnp.int32, (count, 128), 0) == lax.broadcasted_iota(jnp.int32, (count, 128), 1)
    line = jnp.sum(jnp.where(at, total, 0.0), 0, keepdims=True)
    projections[...] = jnp.broadcast_to(line, projections.shape)


def expand(here, there, densities, trial, energies, recycled, devices):
    gvectors = densities.shape[-1]
    vmem = pl.BlockSpec(memory_space=pltpu.VMEM)
    return pl.pallas_call(
        expand_kernel,
        out_shape=[jax.ShapeDtypeStruct(trial.shape, F32), jax.ShapeDtypeStruct((devices, 128), F32)],
        in_specs=[vmem] * 6,
        out_specs=[vmem] * 2,
        compiler_params=pltpu.CompilerParams(vmem_limit_bytes=SMALL_MIB * 2**20),
    )(here, there, densities.reshape(-1, gvectors), trial, energies, recycled)


def finish_kernel(product, recycled, arrived, image, coefficients):
    line = jnp.sum(arrived[...], 0, keepdims=True)
    count = recycled.shape[0]
    coefficients[...] = line[:, :count].reshape(count)
    at = lax.broadcasted_iota(jnp.int32, (count, 128), 0) == lax.broadcasted_iota(jnp.int32, (count, 128), 1)
    column = jnp.sum(jnp.where(at, jnp.broadcast_to(line, (count, 128)), 0.0), 1, keepdims=True)
    span = 512
    for g in range(product.shape[0] // span):
        taken = jnp.sum(recycled[:, g * span:(g + 1) * span] * column, 0, keepdims=True)
        at = pl.ds(g * span, span)
        image[at] = product[at] - taken.reshape(span)


def finish(product, recycled, arrived):
    vmem = pl.BlockSpec(memory_space=pltpu.VMEM)
    return pl.pallas_call(
        finish_kernel,
        out_shape=[jax.ShapeDtypeStruct(product.shape, F32), jax.ShapeDtypeStruct(recycled.shape[:1], F32)],
        in_specs=[vmem] * 3,
        out_specs=[vmem] * 2,
        compiler_params=pltpu.CompilerParams(vmem_limit_bytes=SMALL_MIB * 2**20),
    )(product, recycled, arrived)


def chip_groups(along_row, along_col):
    ids = np.arange(along_row * along_col * 2).reshape(along_row, along_col, 2)
    return [g.tolist() for g in ids[:, :, 0]] + [g.tolist() for g in ids[:, :, 1].T]


def body(trial, energies, densities, screening, pair_index, pair_count, recycled):
    kpoints, transitions, gvectors = densities.shape
    lanes = 128
    per_k = gvectors // lanes
    row_chips = lax.axis_size("zl") * lax.axis_size("x")
    col_chips = lax.axis_size("zh") * lax.axis_size("y")
    cores = lax.axis_size("c")
    col_devices = col_chips * cores
    row_place = lax.axis_index("zl") * lax.axis_size("x") + lax.axis_index("x")
    core = lax.axis_index("c")
    swap = [(0, 1), (1, 0)]
    groups = chip_groups(row_chips, col_chips)

    first_row = jnp.reshape(row_place * col_devices * kpoints, (1,)).astype(jnp.int32)
    local_dens = project(trial, densities)
    from_other = lax.ppermute(local_dens, "c", swap)
    place = core.reshape(1).astype(jnp.int32)
    out = jax.ShapeDtypeStruct((row_chips, 2 * local_dens.shape[0], lanes), BF16)
    index = jax.ShapeDtypeStruct(pair_index.shape[1:], jnp.int32)
    spread, rows, cols = local_call(
        functools.partial(pack_kernel, kpoints, col_devices * kpoints), [out, index, index],
        place, first_row, local_dens, from_other, pair_index, scalars=2, flops=12 * 10**9)
    mine = lax.all_to_all(spread, AXES, 0, 0, axis_index_groups=groups).reshape(-1, lanes)
    theirs = lax.ppermute(mine, "c", swap)

    keep, send = pair_terms(rows, cols, pair_count, place, screening, mine, theirs)

    got = lax.ppermute(send, "c", swap)
    total = local_call(add_kernel, jax.ShapeDtypeStruct(keep.shape, BF16), keep, got)
    parts = lax.all_to_all(
        total.reshape(row_chips, -1, lanes), AXES, 0, 0, axis_index_groups=groups)
    part = jax.ShapeDtypeStruct((kpoints * per_k, lanes), F32)
    here, there = local_call(sum_kernel, [part, part], place, parts, scalars=1)
    devices = row_chips * col_devices
    product, projections = expand(
        here, lax.ppermute(there, "c", swap), densities, trial, energies, recycled, devices)
    arrived = lax.all_to_all(projections, AXES, 0, 0, tiled=True)
    return tuple(finish(product, recycled, arrived))


def solution(mesh):
    fine = Mesh(mesh.devices.reshape(2, 4, 2, 4, 2), AXES)
    placed = (
        P(AXES),
        P(AXES),
        P(AXES, None, None),
        P(AXES, None),
        P(None, AXES),
        P(AXES),
        P(None, AXES),
    )
    return jax.shard_map(
        body, mesh=fine, in_specs=placed, out_specs=(P(AXES), P()), check_vma=False
    )
```

```python
import functools

import jax
import jax.numpy as jnp
import numpy as np
from jax import lax
from jax.experimental import pallas as pl
from jax.experimental.pallas import tpu as pltpu
from jax.sharding import Mesh, PartitionSpec as P

AXES = ("zl", "x", "zh", "y", "c")
F32 = jnp.float32
BF16 = jnp.bfloat16
COPIES = 4
SLOT_MIB = 40
SMALL_MIB = 6
STEP = 32


def slot_kernel(row_index, col_index, count, place, weights, mine, theirs, keep, send,
                rows, cols, sem, even, odd, rest, *tables):
    fetches = [pltpu.make_async_copy(row_index, rows, sem.at[0]),
               pltpu.make_async_copy(col_index, cols, sem.at[1])]
    for fetch in fetches:
        fetch.start()
    row_tables, col_tables = tables[:COPIES], tables[COPIES:]
    live, core = count[0], place[0]
    last = weights.shape[0] - STEP
    zeros = jnp.zeros((4, 128), F32)

    half = mine.shape[0] // 2
    block = half // (mine.shape[0] // 512)

    def fill(source, tables, count, dens_first, at):
        def step(i, _):
            part = source[pl.ds(pl.multiple_of(at(i), 16), 16), :].astype(F32)
            for t in range(4):
                dens = part[4 * t:4 * t + 4]
                entry = jnp.concatenate([dens, zeros] if dens_first else [zeros, dens], 0)
                for table in tables:
                    table[pl.ds(pl.multiple_of((i * 4 + t) * 8, 8), 8), :] = entry
            return 0

        lax.fori_loop(0, count // 16, step, 0, unroll=16)

    def whole(i):
        return i * 16

    def one_core(which):
        per = block // 16
        return lambda i: (i // per) * (2 * block) + which * block + (i % per) * 16

    @pl.when(core == 0)
    def _():
        fill(mine, row_tables, 2 * half, True, whole)
        fill(theirs, col_tables, half, False, one_core(0))

    @pl.when(core != 0)
    def _():
        fill(theirs, row_tables, 2 * half, True, whole)
        fill(mine, col_tables, half, False, one_core(1))

    low = lax.broadcasted_iota(jnp.int32, (8, 128), 0) >= 4

    def one(slot, which, row_weight, col_weight):
        r = pl.ds(pl.multiple_of(rows[slot], 8), 8)
        c = pl.ds(pl.multiple_of(cols[slot], 8), 8)
        row_entry = row_tables[which][r, :]
        col_entry = col_tables[which][c, :]
        row_tables[which][r, :] = row_entry + row_weight * col_entry
        col_tables[which][c, :] = col_entry + col_weight * row_entry

    def spread(first, target, at):
        for g in range(STEP // 16):
            v = weights[pl.ds(pl.multiple_of(first + g * 16, 16), 16), :].astype(F32)
            for h in range(2):
                for j in range(4):
                    target[pl.ds(at + g * 64 + h * 32 + j * 8, 8), :] = v[8 * h:8 * h + 8, 128 * j:128 * j + 128]

    def many(first, source):
        for g in range(STEP // 16):
            for u in range(8):
                slot = first + g * 16 + u
                both = source[pl.ds(g * 64 + u, 8, stride=8), :]
                turned = jnp.concatenate([both[4:8], both[0:4]], 0)
                one(slot, (2 * u) % COPIES, jnp.where(low, turned, 0.0), jnp.where(low, 0.0, both))
                one(slot + 8, (2 * u + 1) % COPIES, jnp.where(low, both, 0.0), jnp.where(low, 0.0, turned))

    for fetch in fetches:
        fetch.wait()
    pairs = live // (2 * STEP)
    spread(0, even, 0)

    def pair(i, _):
        first = i * (2 * STEP)
        spread(first + STEP, odd, 0)
        many(first, even)
        spread(jnp.minimum(first + 2 * STEP, last), even, 0)
        many(first + STEP, odd)
        return 0

    lax.fori_loop(0, pairs, pair, 0)
    done = pairs * (2 * STEP)
    spread(jnp.minimum(done, last - STEP), rest, 0)
    spread(jnp.minimum(done + STEP, last), rest, 4 * STEP)

    def tail(slot, _):
        w = rest[pl.ds(slot // 8 * 32 + slot % 8, 4, stride=8), :]
        w = jnp.concatenate([w, w], 0)
        one(done + slot, 0, jnp.where(low, w, 0.0), jnp.where(low, 0.0, w))
        return 0

    lax.fori_loop(0, live - done, tail, 0)

    def drain(tables, target, count, at, offset):
        def step(i, _):
            parts = []
            for t in range(4):
                entry = pl.ds(pl.multiple_of((i * 4 + t) * 8, 8), 8)
                total = tables[0][entry, :]
                for table in tables[1:]:
                    total = total + table[entry, :]
                parts.append(total[offset:offset + 4])
            rows16 = pl.ds(pl.multiple_of(at(i), 16), 16)
            target[rows16, :] = jnp.concatenate(parts, 0).astype(BF16)
            return 0

        lax.fori_loop(0, count // 16, step, 0, unroll=16)

    def clear(target, at):
        def step(i, _):
            target[pl.ds(pl.multiple_of(at(i), 16), 16), :] = jnp.zeros((16, 128), BF16)
            return 0

        lax.fori_loop(0, half // 16, step, 0, unroll=8)

    @pl.when(core == 0)
    def _():
        drain(row_tables, keep, 2 * half, whole, 4)
        drain(col_tables, send, half, one_core(0), 0)
        clear(send, one_core(1))

    @pl.when(core != 0)
    def _():
        drain(row_tables, send, 2 * half, whole, 4)
        drain(col_tables, keep, half, one_core(1), 0)
        clear(keep, one_core(0))


def pair_terms(rows, cols, count, place, weights, mine, theirs):
    smem = pl.BlockSpec(memory_space=pltpu.SMEM)
    vmem = pl.BlockSpec(memory_space=pltpu.VMEM)
    row_table = pltpu.VMEM((2 * mine.shape[0], 128), F32)
    col_table = pltpu.VMEM((mine.shape[0], 128), F32)
    return pl.pallas_call(
        slot_kernel,
        out_shape=[jax.ShapeDtypeStruct(mine.shape, BF16)] * 2,
        in_specs=[pl.BlockSpec(memory_space=pl.ANY)] * 2 + [smem] * 2 + [vmem] * 3,
        out_specs=[vmem, vmem],
        scratch_shapes=[
            *[pltpu.SMEM(rows.shape, jnp.int32)] * 2, pltpu.SemaphoreType.DMA((2,)),
            *[pltpu.VMEM((STEP * 4, 128), F32)] * 2, pltpu.VMEM((STEP * 8, 128), F32),
            *[row_table] * COPIES, *[col_table] * COPIES],
        compiler_params=pltpu.CompilerParams(vmem_limit_bytes=SLOT_MIB * 2**20),
    )(rows, cols, count, place, weights, mine, theirs)


def local_call(kernel, outs, *args, scalars=0, flops=0):
    smem = pl.BlockSpec(memory_space=pltpu.SMEM)
    vmem = pl.BlockSpec(memory_space=pltpu.VMEM)
    return pl.pallas_call(
        kernel,
        out_shape=outs,
        in_specs=[smem] * scalars + [vmem] * (len(args) - scalars),
        out_specs=jax.tree.map(lambda _: vmem, outs),
        cost_estimate=pl.CostEstimate(flops=flops, bytes_accessed=0, transcendentals=0) if flops else None,
        compiler_params=pltpu.CompilerParams(vmem_limit_bytes=SMALL_MIB * 2**20),
    )(*args)


def pack_kernel(kpoints, spans, place, first_row, local, other, pair_index, out, rows, cols):
    index = pair_index[...]
    rows[...] = ((index[0:1, :] - first_row[0]) * 8).reshape(rows.shape)
    col = index[1:2, :]
    cols[...] = ((col // spans * kpoints + col % kpoints) * 8).reshape(cols.shape)
    size = local.shape[0]

    def step(i, _):
        at = pl.ds(pl.multiple_of(i * 16, 16), 16)
        first, second = local[at, :], other[at, :]
        swapped = place[0] != 0
        low = jnp.where(swapped, second.astype(F32), first.astype(F32)).astype(BF16)
        high = jnp.where(swapped, first.astype(F32), second.astype(F32)).astype(BF16)
        for n in range(out.shape[0]):
            out[n, at, :] = low
            out[n, pl.ds(pl.multiple_of(size + i * 16, 16), 16), :] = high
        return 0

    lax.fori_loop(0, size // 16, step, 0, unroll=2)


def add_kernel(keep, got, out):
    def step(i, _):
        at = pl.ds(pl.multiple_of(i * 16, 16), 16)
        out[at, :] = (keep[at, :].astype(F32) + got[at, :].astype(F32)).astype(BF16)
        return 0

    lax.fori_loop(0, keep.shape[0] // 16, step, 0, unroll=8)


def sum_kernel(place, parts, here, there):
    size = here.shape[0]

    def step(i, _):
        at = pl.ds(pl.multiple_of(i * 16, 16), 16)
        for target, which in ((here, place[0]), (there, 1 - place[0])):
            first = pl.ds(pl.multiple_of(which * size + i * 16, 16), 16)
            total = parts[0, first, :].astype(F32)
            for n in range(1, parts.shape[0]):
                total = total + parts[n, first, :].astype(F32)
            target[at, :] = total
        return 0

    lax.fori_loop(0, size // 16, step, 0, unroll=4)


def project_kernel(trial, densities, out, wide):
    kpoints = out.shape[0] // 4
    span = densities.shape[0] * 8 // kpoints
    rows8 = lax.broadcasted_iota(jnp.int32, (8, span), 0)
    owner = lax.broadcasted_iota(jnp.int32, (8, span), 1) // (span // 8)
    for g in range(kpoints // 8):
        line = jnp.broadcast_to(trial[g * span:(g + 1) * span].reshape(1, span), (8, span))
        left = jnp.where(rows8 == owner, line, 0.0).astype(BF16)
        dens = jnp.dot(left, densities[g * span:(g + 1) * span, :], preferred_element_type=F32)
        for j in range(4):
            wide[pl.ds(32 * g + j, 8, stride=4), :] = dens[:, 128 * j:128 * j + 128]
    out[...] = wide[...].astype(BF16)


def project(trial, densities):
    kpoints, transitions, gvectors = densities.shape
    vmem = pl.BlockSpec(memory_space=pltpu.VMEM)
    return pl.pallas_call(
        project_kernel,
        out_shape=jax.ShapeDtypeStruct((kpoints * 4, 128), BF16),
        in_specs=[vmem, vmem],
        out_specs=vmem,
        scratch_shapes=[pltpu.VMEM((kpoints * 4, 128), F32)],
        cost_estimate=pl.CostEstimate(flops=4 * 10**9, bytes_accessed=0, transcendentals=0),
        compiler_params=pltpu.CompilerParams(vmem_limit_bytes=SMALL_MIB * 2**20),
    )(trial, densities.reshape(-1, gvectors))


def expand_kernel(here, there, densities, trial, energies, recycled, product, projections):
    kpoints = here.shape[0] // 4
    span = densities.shape[0] * 8 // kpoints
    rows8 = lax.broadcasted_iota(jnp.int32, (8, span), 0)
    owner = lax.broadcasted_iota(jnp.int32, (8, span), 1) // (span // 8)
    sums = jnp.zeros((recycled.shape[0], 128), F32)
    for g in range(kpoints // 8):
        field = []
        for j in range(4):
            at = pl.ds(32 * g + j, 8, stride=4)
            field.append(here[at, :] + there[at, :])
        every = lax.dot_general(
            jnp.concatenate(field, 1).astype(BF16), densities[g * span:(g + 1) * span, :],
            (((1,), (1,)), ((), ())), preferred_element_type=F32)
        part = jnp.sum(jnp.where(rows8 == owner, every, 0.0), 0, keepdims=True)
        at = pl.ds(g * span, span)
        line = (energies[at] * trial[at]).reshape(1, span) + part
        product[at] = line.reshape(span)
        weighted = recycled[:, g * span:(g + 1) * span] * line
        for j in range(span // 128):
            sums = sums + weighted[:, 128 * j:128 * j + 128]
    total = jnp.sum(sums, 1, keepdims=True)
    count = total.shape[0]
    at = lax.broadcasted_iota(jnp.int32, (count, 128), 0) == lax.broadcasted_iota(jnp.int32, (count, 128), 1)
    line = jnp.sum(jnp.where(at, total, 0.0), 0, keepdims=True)
    projections[...] = jnp.broadcast_to(line, projections.shape)


def expand(here, there, densities, trial, energies, recycled, devices):
    gvectors = densities.shape[-1]
    vmem = pl.BlockSpec(memory_space=pltpu.VMEM)
    return pl.pallas_call(
        expand_kernel,
        out_shape=[jax.ShapeDtypeStruct(trial.shape, F32), jax.ShapeDtypeStruct((devices, 128), F32)],
        in_specs=[vmem] * 6,
        out_specs=[vmem] * 2,
        compiler_params=pltpu.CompilerParams(vmem_limit_bytes=SMALL_MIB * 2**20),
    )(here, there, densities.reshape(-1, gvectors), trial, energies, recycled)


def finish_kernel(product, recycled, arrived, image, coefficients):
    line = jnp.sum(arrived[...], 0, keepdims=True)
    count = recycled.shape[0]
    coefficients[...] = line[:, :count].reshape(count)
    at = lax.broadcasted_iota(jnp.int32, (count, 128), 0) == lax.broadcasted_iota(jnp.int32, (count, 128), 1)
    column = jnp.sum(jnp.where(at, jnp.broadcast_to(line, (count, 128)), 0.0), 1, keepdims=True)
    span = 512
    for g in range(product.shape[0] // span):
        taken = jnp.sum(recycled[:, g * span:(g + 1) * span] * column, 0, keepdims=True)
        at = pl.ds(g * span, span)
        image[at] = product[at] - taken.reshape(span)


def finish(product, recycled, arrived):
    vmem = pl.BlockSpec(memory_space=pltpu.VMEM)
    return pl.pallas_call(
        finish_kernel,
        out_shape=[jax.ShapeDtypeStruct(product.shape, F32), jax.ShapeDtypeStruct(recycled.shape[:1], F32)],
        in_specs=[vmem] * 3,
        out_specs=[vmem] * 2,
        compiler_params=pltpu.CompilerParams(vmem_limit_bytes=SMALL_MIB * 2**20),
    )(product, recycled, arrived)


def chip_groups(along_row, along_col):
    ids = np.arange(along_row * along_col * 2).reshape(along_row, along_col, 2)
    return [g.tolist() for g in ids[:, :, 0]] + [g.tolist() for g in ids[:, :, 1].T]


def body(trial, energies, densities, screening, pair_index, pair_count, recycled):
    kpoints, transitions, gvectors = densities.shape
    lanes = 128
    per_k = gvectors // lanes
    row_chips = lax.axis_size("zl") * lax.axis_size("x")
    col_chips = lax.axis_size("zh") * lax.axis_size("y")
    cores = lax.axis_size("c")
    col_devices = col_chips * cores
    row_place = lax.axis_index("zl") * lax.axis_size("x") + lax.axis_index("x")
    core = lax.axis_index("c")
    swap = [(0, 1), (1, 0)]
    groups = chip_groups(row_chips, col_chips)

    first_row = jnp.reshape(row_place * col_devices * kpoints, (1,)).astype(jnp.int32)
    local_dens = project(trial, densities)
    from_other = lax.ppermute(local_dens, "c", swap)
    place = core.reshape(1).astype(jnp.int32)
    out = jax.ShapeDtypeStruct((row_chips, 2 * local_dens.shape[0], lanes), BF16)
    index = jax.ShapeDtypeStruct(pair_index.shape[1:], jnp.int32)
    spread, rows, cols = local_call(
        functools.partial(pack_kernel, kpoints, col_devices * kpoints), [out, index, index],
        place, first_row, local_dens, from_other, pair_index, scalars=2, flops=12 * 10**9)
    mine = lax.all_to_all(spread, AXES, 0, 0, axis_index_groups=groups).reshape(-1, lanes)
    theirs = lax.ppermute(mine, "c", swap)

    keep, send = pair_terms(rows, cols, pair_count, place, screening, mine, theirs)

    got = lax.ppermute(send, "c", swap)
    total = local_call(add_kernel, jax.ShapeDtypeStruct(keep.shape, BF16), keep, got)
    parts = lax.all_to_all(
        total.reshape(row_chips, -1, lanes), AXES, 0, 0, axis_index_groups=groups)
    part = jax.ShapeDtypeStruct((kpoints * per_k, lanes), F32)
    here, there = local_call(sum_kernel, [part, part], place, parts, scalars=1)
    devices = row_chips * col_devices
    product, projections = expand(
        here, lax.ppermute(there, "c", swap), densities, trial, energies, recycled, devices)
    arrived = lax.all_to_all(projections, AXES, 0, 0, tiled=True)
    return tuple(finish(product, recycled, arrived))


def solution(mesh):
    fine = Mesh(mesh.devices.reshape(2, 4, 2, 4, 2), AXES)
    placed = (
        P(AXES),
        P(AXES),
        P(AXES, None, None),
        P(AXES, None),
        P(None, AXES),
        P(AXES),
        P(None, AXES),
    )
    return jax.shard_map(
        body, mesh=fine, in_specs=placed, out_specs=(P(AXES), P()), check_vma=False
    )
```

```python
import functools

import jax
import jax.numpy as jnp
import numpy as np
from jax import lax
from jax.experimental import pallas as pl
from jax.experimental.pallas import tpu as pltpu
from jax.sharding import Mesh, PartitionSpec as P

AXES = ("zl", "x", "zh", "y", "c")
F32 = jnp.float32
BF16 = jnp.bfloat16
COPIES = 4
SLOT_MIB = 48
SMALL_MIB = 6
DIAG_FLOPS = 4 * 10**9
STEP = 32
CHUNK = 2048
FIRST = 2048


def slot_kernel(row_index, col_index, count, place, weights, mine, theirs, keep, send,
                rows, cols, sem, part, part_sem, even, odd, rest, *tables):
    fetches = [pltpu.make_async_copy(row_index, rows, sem.at[0]),
               pltpu.make_async_copy(col_index, cols, sem.at[1])]
    for fetch in fetches:
        fetch.start()
    row_tables, col_tables = tables[:COPIES], tables[COPIES:]
    live, core = count[0], place[0]

    def part_copy(i):
        at = pl.ds(pl.multiple_of(i * CHUNK, CHUNK), CHUNK)
        return pltpu.make_async_copy(weights.at[at], part.at[at], part_sem.at[i])

    def part_start(i, _):
        part_copy(i).start()
        return 0

    lax.fori_loop(0, (live + CHUNK - 1) // CHUNK, part_start, 0)
    zeros = jnp.zeros((4, 128), F32)

    half = mine.shape[0] // 2
    block = half // (mine.shape[0] // 512)

    def fill(source, tables, count, dens_first, at):
        def step(i, _):
            part = source[pl.ds(pl.multiple_of(at(i), 16), 16), :].astype(F32)
            for t in range(4):
                dens = part[4 * t:4 * t + 4]
                entry = jnp.concatenate([dens, zeros] if dens_first else [zeros, dens], 0)
                for table in tables:
                    table[pl.ds(pl.multiple_of((i * 4 + t) * 8, 8), 8), :] = entry
            return 0

        lax.fori_loop(0, count // 16, step, 0, unroll=16)

    def whole(i):
        return i * 16

    def one_core(which):
        per = block // 16
        return lambda i: (i // per) * (2 * block) + which * block + (i % per) * 16

    @pl.when(core == 0)
    def _():
        fill(mine, row_tables, 2 * half, True, whole)
        fill(theirs, col_tables, half, False, one_core(0))

    @pl.when(core != 0)
    def _():
        fill(theirs, row_tables, 2 * half, True, whole)
        fill(mine, col_tables, half, False, one_core(1))

    low = lax.broadcasted_iota(jnp.int32, (8, 128), 0) >= 4

    def one(slot, which, row_weight, col_weight):
        r = pl.ds(pl.multiple_of(rows[slot], 8), 8)
        c = pl.ds(pl.multiple_of(cols[slot], 8), 8)
        row_entry = row_tables[which][r, :]
        col_entry = col_tables[which][c, :]
        row_tables[which][r, :] = row_entry + row_weight * col_entry
        col_tables[which][c, :] = col_entry + col_weight * row_entry

    def spread(first, target, at):
        for g in range(STEP // 16):
            v = part[pl.ds(pl.multiple_of(first + g * 16, 16), 16), :].astype(F32)
            for h in range(2):
                for j in range(4):
                    target[pl.ds(at + g * 64 + h * 32 + j * 8, 8), :] = v[8 * h:8 * h + 8, 128 * j:128 * j + 128]

    def many(first, source):
        for g in range(STEP // 16):
            for u in range(8):
                slot = first + g * 16 + u
                both = source[pl.ds(g * 64 + u, 8, stride=8), :]
                turned = jnp.concatenate([both[4:8], both[0:4]], 0)
                one(slot, (2 * u) % COPIES, jnp.where(low, turned, 0.0), jnp.where(low, 0.0, both))
                one(slot + 8, (2 * u + 1) % COPIES, jnp.where(low, both, 0.0), jnp.where(low, 0.0, turned))

    for fetch in fetches:
        fetch.wait()
    pairs = live // (2 * STEP)

    def pair(i, end):
        first = i * (2 * STEP)
        spread(first + STEP, odd, 0)
        many(first, even)
        spread(jnp.minimum(first + 2 * STEP, end * (2 * STEP) - STEP), even, 0)
        many(first + STEP, odd)
        return end

    def phase(n, _):
        begin = n * (FIRST // (2 * STEP))
        end = jnp.where(n == 0, jnp.minimum(pairs, FIRST // (2 * STEP)), pairs)

        def part_wait(i, _):
            part_copy(i).wait()
            return 0

        arrived = jnp.where(n == 0, jnp.minimum(live, FIRST), live)
        lax.fori_loop(n * (FIRST // CHUNK), (arrived + CHUNK - 1) // CHUNK, part_wait, 0)
        spread(begin * (2 * STEP), even, 0)
        lax.fori_loop(begin, end, pair, end)
        return 0

    lax.fori_loop(0, jnp.where(live > FIRST, 2, 1), phase, 0)
    done = pairs * (2 * STEP)
    @pl.when(live > done)
    def _():
        spread(done, rest, 0)
        spread(done + STEP, rest, 4 * STEP)

    def tail(slot, _):
        w = rest[pl.ds(slot // 8 * 32 + slot % 8, 4, stride=8), :]
        w = jnp.concatenate([w, w], 0)
        one(done + slot, 0, jnp.where(low, w, 0.0), jnp.where(low, 0.0, w))
        return 0

    lax.fori_loop(0, live - done, tail, 0)

    def drain(tables, target, count, at, offset):
        def step(i, _):
            parts = []
            for t in range(4):
                entry = pl.ds(pl.multiple_of((i * 4 + t) * 8, 8), 8)
                total = tables[0][entry, :]
                for table in tables[1:]:
                    total = total + table[entry, :]
                parts.append(total[offset:offset + 4])
            rows16 = pl.ds(pl.multiple_of(at(i), 16), 16)
            target[rows16, :] = jnp.concatenate(parts, 0).astype(BF16)
            return 0

        lax.fori_loop(0, count // 16, step, 0, unroll=16)

    def clear(target, at):
        def step(i, _):
            target[pl.ds(pl.multiple_of(at(i), 16), 16), :] = jnp.zeros((16, 128), BF16)
            return 0

        lax.fori_loop(0, half // 16, step, 0, unroll=8)

    @pl.when(core == 0)
    def _():
        drain(row_tables, keep, 2 * half, whole, 4)
        drain(col_tables, send, half, one_core(0), 0)
        clear(send, one_core(1))

    @pl.when(core != 0)
    def _():
        drain(row_tables, send, 2 * half, whole, 4)
        drain(col_tables, keep, half, one_core(1), 0)
        clear(keep, one_core(0))


def pair_terms(rows, cols, count, place, weights, mine, theirs):
    smem = pl.BlockSpec(memory_space=pltpu.SMEM)
    vmem = pl.BlockSpec(memory_space=pltpu.VMEM)
    hold = pl.BlockSpec(memory_space=pl.ANY)
    row_table = pltpu.VMEM((2 * mine.shape[0], 128), F32)
    col_table = pltpu.VMEM((mine.shape[0], 128), F32)
    return pl.pallas_call(
        slot_kernel,
        out_shape=[jax.ShapeDtypeStruct(mine.shape, BF16)] * 2,
        in_specs=[hold] * 2 + [smem] * 2 + [hold, vmem, vmem],
        out_specs=[vmem, vmem],
        scratch_shapes=[
            *[pltpu.SMEM(rows.shape, jnp.int32)] * 2, pltpu.SemaphoreType.DMA((2,)),
            pltpu.VMEM(weights.shape, BF16), pltpu.SemaphoreType.DMA((weights.shape[0] // CHUNK,)),
            *[pltpu.VMEM((STEP * 4, 128), F32)] * 2, pltpu.VMEM((STEP * 8, 128), F32),
            *[row_table] * COPIES, *[col_table] * COPIES],
        compiler_params=pltpu.CompilerParams(vmem_limit_bytes=SLOT_MIB * 2**20),
    )(rows, cols, count, place, weights, mine, theirs)


def local_call(kernel, outs, *args, scalars=0, flops=0):
    smem = pl.BlockSpec(memory_space=pltpu.SMEM)
    vmem = pl.BlockSpec(memory_space=pltpu.VMEM)
    return pl.pallas_call(
        kernel,
        out_shape=outs,
        in_specs=[smem] * scalars + [vmem] * (len(args) - scalars),
        out_specs=jax.tree.map(lambda _: vmem, outs),
        cost_estimate=pl.CostEstimate(flops=flops, bytes_accessed=0, transcendentals=0) if flops else None,
        compiler_params=pltpu.CompilerParams(vmem_limit_bytes=SMALL_MIB * 2**20),
    )(*args)


def pack_kernel(kpoints, spans, place, first_row, local, other, pair_index, out, rows, cols):
    index = pair_index[...]
    rows[...] = ((index[0:1, :] - first_row[0]) * 8).reshape(rows.shape)
    col = index[1:2, :]
    cols[...] = ((col // spans * kpoints + col % kpoints) * 8).reshape(cols.shape)
    size = local.shape[0]

    def step(i, _):
        at = pl.ds(pl.multiple_of(i * 16, 16), 16)
        first, second = local[at, :], other[at, :]
        swapped = place[0] != 0
        low = jnp.where(swapped, second.astype(F32), first.astype(F32)).astype(BF16)
        high = jnp.where(swapped, first.astype(F32), second.astype(F32)).astype(BF16)
        for n in range(out.shape[0]):
            out[n, at, :] = low
            out[n, pl.ds(pl.multiple_of(size + i * 16, 16), 16), :] = high
        return 0

    lax.fori_loop(0, size // 16, step, 0, unroll=2)


def add_kernel(keep, got, out):
    def step(i, _):
        at = pl.ds(pl.multiple_of(i * 16, 16), 16)
        out[at, :] = (keep[at, :].astype(F32) + got[at, :].astype(F32)).astype(BF16)
        return 0

    lax.fori_loop(0, keep.shape[0] // 16, step, 0, unroll=8)


def sum_kernel(place, parts, here, there):
    size = here.shape[0]

    def step(i, _):
        at = pl.ds(pl.multiple_of(i * 16, 16), 16)
        for target, which in ((here, place[0]), (there, 1 - place[0])):
            first = pl.ds(pl.multiple_of(which * size + i * 16, 16), 16)
            total = parts[0, first, :].astype(F32)
            for n in range(1, parts.shape[0]):
                total = total + parts[n, first, :].astype(F32)
            target[at, :] = total
        return 0

    lax.fori_loop(0, size // 16, step, 0, unroll=4)


def diagonal_kernel(trial, out):
    span = out.shape[1]
    rows8 = lax.broadcasted_iota(jnp.int32, (8, span), 0)
    owner = lax.broadcasted_iota(jnp.int32, (8, span), 1) // (span // 8)
    for g in range(out.shape[0] // 16):
        both = []
        for n in (2 * g, 2 * g + 1):
            line = jnp.broadcast_to(trial[n * span:(n + 1) * span].reshape(1, span), (8, span))
            both.append(jnp.where(rows8 == owner, line, 0.0))
        out[16 * g:16 * g + 16, :] = jnp.concatenate(both, 0).astype(BF16)


def project_kernel(diagonal, densities, out, wide):
    kpoints, span = diagonal.shape
    for g in range(kpoints // 16):
        pair = diagonal[16 * g:16 * g + 16, :]
        for h in range(2):
            n = 2 * g + h
            dens = jnp.dot(pair[8 * h:8 * h + 8, :], densities[n * span:(n + 1) * span, :], preferred_element_type=F32)
            for j in range(4):
                wide[pl.ds(32 * n + j, 8, stride=4), :] = dens[:, 128 * j:128 * j + 128]
    out[...] = wide[...].astype(BF16)


def project(trial, densities):
    kpoints, transitions, gvectors = densities.shape
    vmem = pl.BlockSpec(memory_space=pltpu.VMEM)
    diagonal = local_call(
        diagonal_kernel, jax.ShapeDtypeStruct((kpoints, 8 * transitions), BF16), trial, flops=DIAG_FLOPS)
    return pl.pallas_call(
        project_kernel,
        out_shape=jax.ShapeDtypeStruct((kpoints * 4, 128), BF16),
        in_specs=[vmem, vmem],
        out_specs=vmem,
        scratch_shapes=[pltpu.VMEM((kpoints * 4, 128), F32)],
        cost_estimate=pl.CostEstimate(flops=4 * 10**9, bytes_accessed=0, transcendentals=0),
        compiler_params=pltpu.CompilerParams(vmem_limit_bytes=SMALL_MIB * 2**20),
    )(diagonal, densities.reshape(-1, gvectors))


def expand_kernel(here, there, densities, trial, energies, recycled, product, projections):
    kpoints = here.shape[0] // 4
    span = densities.shape[0] * 8 // kpoints
    rows8 = lax.broadcasted_iota(jnp.int32, (8, span), 0)
    owner = lax.broadcasted_iota(jnp.int32, (8, span), 1) // (span // 8)
    sums = jnp.zeros((recycled.shape[0], 128), F32)
    for g in range(kpoints // 8):
        field = []
        for j in range(4):
            at = pl.ds(32 * g + j, 8, stride=4)
            field.append(here[at, :] + there[at, :])
        every = lax.dot_general(
            jnp.concatenate(field, 1).astype(BF16), densities[g * span:(g + 1) * span, :],
            (((1,), (1,)), ((), ())), preferred_element_type=F32)
        part = jnp.sum(jnp.where(rows8 == owner, every, 0.0), 0, keepdims=True)
        at = pl.ds(g * span, span)
        line = (energies[at] * trial[at]).reshape(1, span) + part
        product[at] = line.reshape(span)
        weighted = recycled[:, g * span:(g + 1) * span] * line
        for j in range(span // 128):
            sums = sums + weighted[:, 128 * j:128 * j + 128]
    total = jnp.sum(sums, 1, keepdims=True)
    count = total.shape[0]
    at = lax.broadcasted_iota(jnp.int32, (count, 128), 0) == lax.broadcasted_iota(jnp.int32, (count, 128), 1)
    line = jnp.sum(jnp.where(at, total, 0.0), 0, keepdims=True)
    projections[...] = jnp.broadcast_to(line, projections.shape)


def expand(here, there, densities, trial, energies, recycled, devices):
    gvectors = densities.shape[-1]
    vmem = pl.BlockSpec(memory_space=pltpu.VMEM)
    return pl.pallas_call(
        expand_kernel,
        out_shape=[jax.ShapeDtypeStruct(trial.shape, F32), jax.ShapeDtypeStruct((devices, 128), F32)],
        in_specs=[vmem] * 6,
        out_specs=[vmem] * 2,
        compiler_params=pltpu.CompilerParams(vmem_limit_bytes=SMALL_MIB * 2**20),
    )(here, there, densities.reshape(-1, gvectors), trial, energies, recycled)


def finish_kernel(product, recycled, arrived, image, coefficients):
    line = jnp.sum(arrived[...], 0, keepdims=True)
    count = recycled.shape[0]
    coefficients[...] = line[:, :count].reshape(count)
    at = lax.broadcasted_iota(jnp.int32, (count, 128), 0) == lax.broadcasted_iota(jnp.int32, (count, 128), 1)
    column = jnp.sum(jnp.where(at, jnp.broadcast_to(line, (count, 128)), 0.0), 1, keepdims=True)
    span = 512
    for g in range(product.shape[0] // span):
        taken = jnp.sum(recycled[:, g * span:(g + 1) * span] * column, 0, keepdims=True)
        at = pl.ds(g * span, span)
        image[at] = product[at] - taken.reshape(span)


def finish(product, recycled, arrived):
    vmem = pl.BlockSpec(memory_space=pltpu.VMEM)
    return pl.pallas_call(
        finish_kernel,
        out_shape=[jax.ShapeDtypeStruct(product.shape, F32), jax.ShapeDtypeStruct(recycled.shape[:1], F32)],
        in_specs=[vmem] * 3,
        out_specs=[vmem] * 2,
        compiler_params=pltpu.CompilerParams(vmem_limit_bytes=SMALL_MIB * 2**20),
    )(product, recycled, arrived)


def chip_groups(along_row, along_col):
    ids = np.arange(along_row * along_col * 2).reshape(along_row, along_col, 2)
    return [g.tolist() for g in ids[:, :, 0]] + [g.tolist() for g in ids[:, :, 1].T]


def body(trial, energies, densities, screening, pair_index, pair_count, recycled):
    kpoints, transitions, gvectors = densities.shape
    lanes = 128
    per_k = gvectors // lanes
    row_chips = lax.axis_size("zl") * lax.axis_size("x")
    col_chips = lax.axis_size("zh") * lax.axis_size("y")
    cores = lax.axis_size("c")
    col_devices = col_chips * cores
    row_place = lax.axis_index("zl") * lax.axis_size("x") + lax.axis_index("x")
    core = lax.axis_index("c")
    swap = [(0, 1), (1, 0)]
    groups = chip_groups(row_chips, col_chips)

    first_row = jnp.reshape(row_place * col_devices * kpoints, (1,)).astype(jnp.int32)
    local_dens = project(trial, densities)
    from_other = lax.ppermute(local_dens, "c", swap)
    place = core.reshape(1).astype(jnp.int32)
    out = jax.ShapeDtypeStruct((row_chips, 2 * local_dens.shape[0], lanes), BF16)
    index = jax.ShapeDtypeStruct(pair_index.shape[1:], jnp.int32)
    spread, rows, cols = local_call(
        functools.partial(pack_kernel, kpoints, col_devices * kpoints), [out, index, index],
        place, first_row, local_dens, from_other, pair_index, scalars=2)
    mine = lax.all_to_all(spread, AXES, 0, 0, axis_index_groups=groups).reshape(-1, lanes)
    theirs = lax.ppermute(mine, "c", swap)

    keep, send = pair_terms(rows, cols, pair_count, place, screening, mine, theirs)

    got = lax.ppermute(send, "c", swap)
    total = local_call(add_kernel, jax.ShapeDtypeStruct(keep.shape, BF16), keep, got)
    parts = lax.all_to_all(
        total.reshape(row_chips, -1, lanes), AXES, 0, 0, axis_index_groups=groups)
    part = jax.ShapeDtypeStruct((kpoints * per_k, lanes), F32)
    here, there = local_call(sum_kernel, [part, part], place, parts, scalars=1)
    devices = row_chips * col_devices
    product, projections = expand(
        here, lax.ppermute(there, "c", swap), densities, trial, energies, recycled, devices)
    arrived = lax.all_to_all(projections, AXES, 0, 0, tiled=True)
    return tuple(finish(product, recycled, arrived))


def solution(mesh):
    fine = Mesh(mesh.devices.reshape(2, 4, 2, 4, 2), AXES)
    placed = (
        P(AXES),
        P(AXES),
        P(AXES, None, None),
        P(AXES, None),
        P(None, AXES),
        P(AXES),
        P(None, AXES),
    )
    return jax.shard_map(
        body, mesh=fine, in_specs=placed, out_specs=(P(AXES), P()), check_vma=False
    )
```

```python
import functools

import jax
import jax.numpy as jnp
import numpy as np
from jax import lax
from jax.experimental import pallas as pl
from jax.experimental.pallas import tpu as pltpu
from jax.sharding import Mesh, PartitionSpec as P

AXES = ("zl", "x", "zh", "y", "c")
F32 = jnp.float32
BF16 = jnp.bfloat16
COPIES = 4
SLOT_MIB = 48
SMALL_MIB = 6
DIAG_FLOPS = 4 * 10**9
STEP = 32
CHUNK = 2048
FIRST = 2048


def slot_kernel(row_index, col_index, count, place, weights, mine, theirs, keep, send,
                rows, cols, sem, part, part_sem, even, odd, rest, *tables):
    fetches = [pltpu.make_async_copy(row_index, rows, sem.at[0]),
               pltpu.make_async_copy(col_index, cols, sem.at[1])]
    for fetch in fetches:
        fetch.start()
    row_tables, col_tables = tables[:COPIES], tables[COPIES:]
    live, core = count[0], place[0]

    def part_copy(i):
        at = pl.ds(pl.multiple_of(i * CHUNK, CHUNK), CHUNK)
        return pltpu.make_async_copy(weights.at[at], part.at[at], part_sem.at[i])

    def part_start(i, _):
        part_copy(i).start()
        return 0

    lax.fori_loop(0, (live + CHUNK - 1) // CHUNK, part_start, 0)
    zeros = jnp.zeros((4, 128), F32)

    half = mine.shape[0] // 2
    block = half // (mine.shape[0] // 512)

    def fill(source, tables, count, dens_first, at):
        def step(i, _):
            part = source[pl.ds(pl.multiple_of(at(i), 16), 16), :].astype(F32)
            for t in range(4):
                dens = part[4 * t:4 * t + 4]
                entry = jnp.concatenate([dens, zeros] if dens_first else [zeros, dens], 0)
                for table in tables:
                    table[pl.ds(pl.multiple_of((i * 4 + t) * 8, 8), 8), :] = entry
            return 0

        lax.fori_loop(0, count // 16, step, 0, unroll=16)

    def whole(i):
        return i * 16

    def one_core(which):
        per = block // 16
        return lambda i: (i // per) * (2 * block) + which * block + (i % per) * 16

    @pl.when(core == 0)
    def _():
        fill(mine, row_tables, 2 * half, True, whole)
        fill(theirs, col_tables, half, False, one_core(0))

    @pl.when(core != 0)
    def _():
        fill(theirs, row_tables, 2 * half, True, whole)
        fill(mine, col_tables, half, False, one_core(1))

    low = lax.broadcasted_iota(jnp.int32, (8, 128), 0) >= 4

    def one(slot, which, row_weight, col_weight):
        r = pl.ds(pl.multiple_of(rows[slot], 8), 8)
        c = pl.ds(pl.multiple_of(cols[slot], 8), 8)
        row_entry = row_tables[which][r, :]
        col_entry = col_tables[which][c, :]
        row_tables[which][r, :] = row_entry + row_weight * col_entry
        col_tables[which][c, :] = col_entry + col_weight * row_entry

    def spread(first, target, at):
        for g in range(STEP // 16):
            v = part[pl.ds(pl.multiple_of(first + g * 16, 16), 16), :].astype(F32)
            for h in range(2):
                for j in range(4):
                    target[pl.ds(at + g * 64 + h * 32 + j * 8, 8), :] = v[8 * h:8 * h + 8, 128 * j:128 * j + 128]

    def many(first, source):
        for g in range(STEP // 16):
            for u in range(8):
                slot = first + g * 16 + u
                both = source[pl.ds(g * 64 + u, 8, stride=8), :]
                turned = jnp.concatenate([both[4:8], both[0:4]], 0)
                one(slot, (2 * u) % COPIES, jnp.where(low, turned, 0.0), jnp.where(low, 0.0, both))
                one(slot + 8, (2 * u + 1) % COPIES, jnp.where(low, both, 0.0), jnp.where(low, 0.0, turned))

    for fetch in fetches:
        fetch.wait()
    pairs = live // (2 * STEP)

    def pair(i, end):
        first = i * (2 * STEP)
        spread(first + STEP, odd, 0)
        many(first, even)
        spread(jnp.minimum(first + 2 * STEP, end * (2 * STEP) - STEP), even, 0)
        many(first + STEP, odd)
        return end

    def phase(n, _):
        begin = n * (FIRST // (2 * STEP))
        end = jnp.where(n == 0, jnp.minimum(pairs, FIRST // (2 * STEP)), pairs)

        def part_wait(i, _):
            part_copy(i).wait()
            return 0

        arrived = jnp.where(n == 0, jnp.minimum(live, FIRST), live)
        lax.fori_loop(n * (FIRST // CHUNK), (arrived + CHUNK - 1) // CHUNK, part_wait, 0)
        spread(begin * (2 * STEP), even, 0)
        lax.fori_loop(begin, end, pair, end)
        return 0

    lax.fori_loop(0, jnp.where(live > FIRST, 2, 1), phase, 0)
    done = pairs * (2 * STEP)
    @pl.when(live > done)
    def _():
        spread(done, rest, 0)
        spread(done + STEP, rest, 4 * STEP)

    def tail(slot, _):
        w = rest[pl.ds(slot // 8 * 32 + slot % 8, 4, stride=8), :]
        w = jnp.concatenate([w, w], 0)
        one(done + slot, 0, jnp.where(low, w, 0.0), jnp.where(low, 0.0, w))
        return 0

    lax.fori_loop(0, live - done, tail, 0)

    def drain(tables, target, count, at, offset):
        def step(i, _):
            parts = []
            for t in range(4):
                entry = pl.ds(pl.multiple_of((i * 4 + t) * 8, 8), 8)
                total = tables[0][entry, :]
                for table in tables[1:]:
                    total = total + table[entry, :]
                parts.append(total[offset:offset + 4])
            rows16 = pl.ds(pl.multiple_of(at(i), 16), 16)
            target[rows16, :] = jnp.concatenate(parts, 0).astype(BF16)
            return 0

        lax.fori_loop(0, count // 16, step, 0, unroll=16)

    def clear(target, at):
        def step(i, _):
            target[pl.ds(pl.multiple_of(at(i), 16), 16), :] = jnp.zeros((16, 128), BF16)
            return 0

        lax.fori_loop(0, half // 16, step, 0, unroll=8)

    @pl.when(core == 0)
    def _():
        drain(row_tables, keep, 2 * half, whole, 4)
        drain(col_tables, send, half, one_core(0), 0)
        clear(send, one_core(1))

    @pl.when(core != 0)
    def _():
        drain(row_tables, send, 2 * half, whole, 4)
        drain(col_tables, keep, half, one_core(1), 0)
        clear(keep, one_core(0))


def pair_terms(rows, cols, count, place, weights, mine, theirs):
    smem = pl.BlockSpec(memory_space=pltpu.SMEM)
    vmem = pl.BlockSpec(memory_space=pltpu.VMEM)
    hold = pl.BlockSpec(memory_space=pl.ANY)
    row_table = pltpu.VMEM((2 * mine.shape[0], 128), F32)
    col_table = pltpu.VMEM((mine.shape[0], 128), F32)
    return pl.pallas_call(
        slot_kernel,
        out_shape=[jax.ShapeDtypeStruct(mine.shape, BF16)] * 2,
        in_specs=[hold] * 2 + [smem] * 2 + [hold, vmem, vmem],
        out_specs=[vmem, vmem],
        scratch_shapes=[
            *[pltpu.SMEM(rows.shape, jnp.int32)] * 2, pltpu.SemaphoreType.DMA((2,)),
            pltpu.VMEM(weights.shape, BF16), pltpu.SemaphoreType.DMA((weights.shape[0] // CHUNK,)),
            *[pltpu.VMEM((STEP * 4, 128), F32)] * 2, pltpu.VMEM((STEP * 8, 128), F32),
            *[row_table] * COPIES, *[col_table] * COPIES],
        compiler_params=pltpu.CompilerParams(vmem_limit_bytes=SLOT_MIB * 2**20),
    )(rows, cols, count, place, weights, mine, theirs)


def local_call(kernel, outs, *args, scalars=0, flops=0):
    smem = pl.BlockSpec(memory_space=pltpu.SMEM)
    vmem = pl.BlockSpec(memory_space=pltpu.VMEM)
    return pl.pallas_call(
        kernel,
        out_shape=outs,
        in_specs=[smem] * scalars + [vmem] * (len(args) - scalars),
        out_specs=jax.tree.map(lambda _: vmem, outs),
        cost_estimate=pl.CostEstimate(flops=flops, bytes_accessed=0, transcendentals=0) if flops else None,
        compiler_params=pltpu.CompilerParams(vmem_limit_bytes=SMALL_MIB * 2**20),
    )(*args)


def pack_kernel(kpoints, spans, place, first_row, local, other, pair_index, out, rows, cols):
    index = pair_index[...]
    rows[...] = ((index[0:1, :] - first_row[0]) * 8).reshape(rows.shape)
    col = index[1:2, :]
    cols[...] = ((col // spans * kpoints + col % kpoints) * 8).reshape(cols.shape)
    size = local.shape[0]

    def step(i, _):
        at = pl.ds(pl.multiple_of(i * 16, 16), 16)
        first, second = local[at, :], other[at, :]
        swapped = place[0] != 0
        low = jnp.where(swapped, second.astype(F32), first.astype(F32)).astype(BF16)
        high = jnp.where(swapped, first.astype(F32), second.astype(F32)).astype(BF16)
        for n in range(out.shape[0]):
            out[n, at, :] = low
            out[n, pl.ds(pl.multiple_of(size + i * 16, 16), 16), :] = high
        return 0

    lax.fori_loop(0, size // 16, step, 0, unroll=2)


def add_kernel(keep, got, out):
    def step(i, _):
        at = pl.ds(pl.multiple_of(i * 16, 16), 16)
        out[at, :] = (keep[at, :].astype(F32) + got[at, :].astype(F32)).astype(BF16)
        return 0

    lax.fori_loop(0, keep.shape[0] // 16, step, 0, unroll=8)


def sum_kernel(which, parts, out):
    size = out.shape[0]

    def step(i, _):
        first = pl.ds(pl.multiple_of(which[0] * size + i * 16, 16), 16)
        total = parts[0, first, :].astype(F32)
        for n in range(1, parts.shape[0]):
            total = total + parts[n, first, :].astype(F32)
        out[pl.ds(pl.multiple_of(i * 16, 16), 16), :] = total.astype(out.dtype)
        return 0

    lax.fori_loop(0, size // 16, step, 0, unroll=4)


def diagonal_kernel(trial, out):
    span = out.shape[1]
    rows8 = lax.broadcasted_iota(jnp.int32, (8, span), 0)
    owner = lax.broadcasted_iota(jnp.int32, (8, span), 1) // (span // 8)
    for g in range(out.shape[0] // 16):
        both = []
        for n in (2 * g, 2 * g + 1):
            line = jnp.broadcast_to(trial[n * span:(n + 1) * span].reshape(1, span), (8, span))
            both.append(jnp.where(rows8 == owner, line, 0.0))
        out[16 * g:16 * g + 16, :] = jnp.concatenate(both, 0).astype(BF16)


def project_kernel(diagonal, densities, out, wide):
    kpoints, span = diagonal.shape
    for g in range(kpoints // 16):
        pair = diagonal[16 * g:16 * g + 16, :]
        for h in range(2):
            n = 2 * g + h
            dens = jnp.dot(pair[8 * h:8 * h + 8, :], densities[n * span:(n + 1) * span, :], preferred_element_type=F32)
            for j in range(4):
                wide[pl.ds(32 * n + j, 8, stride=4), :] = dens[:, 128 * j:128 * j + 128]
    out[...] = wide[...].astype(BF16)


def project(trial, densities):
    kpoints, transitions, gvectors = densities.shape
    vmem = pl.BlockSpec(memory_space=pltpu.VMEM)
    diagonal = local_call(
        diagonal_kernel, jax.ShapeDtypeStruct((kpoints, 8 * transitions), BF16), trial, flops=DIAG_FLOPS)
    return pl.pallas_call(
        project_kernel,
        out_shape=jax.ShapeDtypeStruct((kpoints * 4, 128), BF16),
        in_specs=[vmem, vmem],
        out_specs=vmem,
        scratch_shapes=[pltpu.VMEM((kpoints * 4, 128), F32)],
        cost_estimate=pl.CostEstimate(flops=4 * 10**9, bytes_accessed=0, transcendentals=0),
        compiler_params=pltpu.CompilerParams(vmem_limit_bytes=SMALL_MIB * 2**20),
    )(diagonal, densities.reshape(-1, gvectors))


def expand_kernel(here, there, densities, trial, energies, recycled, product, projections, field_sum):
    kpoints = here.shape[0] // 4
    span = densities.shape[0] * 8 // kpoints
    rows8 = lax.broadcasted_iota(jnp.int32, (8, span), 0)
    owner = lax.broadcasted_iota(jnp.int32, (8, span), 1) // (span // 8)
    sums = jnp.zeros((recycled.shape[0], 128), F32)
    field_sum[...] = here[...] + there[...].astype(F32)
    for g in range(kpoints // 8):
        field = []
        for j in range(4):
            at = pl.ds(32 * g + j, 8, stride=4)
            field.append(field_sum[at, :])
        every = lax.dot_general(
            jnp.concatenate(field, 1).astype(BF16), densities[g * span:(g + 1) * span, :],
            (((1,), (1,)), ((), ())), preferred_element_type=F32)
        part = jnp.sum(jnp.where(rows8 == owner, every, 0.0), 0, keepdims=True)
        at = pl.ds(g * span, span)
        line = (energies[at] * trial[at]).reshape(1, span) + part
        product[at] = line.reshape(span)
        weighted = recycled[:, g * span:(g + 1) * span] * line
        for j in range(span // 128):
            sums = sums + weighted[:, 128 * j:128 * j + 128]
    total = jnp.sum(sums, 1, keepdims=True)
    count = total.shape[0]
    at = lax.broadcasted_iota(jnp.int32, (count, 128), 0) == lax.broadcasted_iota(jnp.int32, (count, 128), 1)
    line = jnp.sum(jnp.where(at, total, 0.0), 0, keepdims=True)
    projections[...] = jnp.broadcast_to(line, projections.shape)


def expand(here, there, densities, trial, energies, recycled, devices):
    gvectors = densities.shape[-1]
    vmem = pl.BlockSpec(memory_space=pltpu.VMEM)
    return pl.pallas_call(
        expand_kernel,
        out_shape=[jax.ShapeDtypeStruct(trial.shape, F32), jax.ShapeDtypeStruct((devices, 128), F32)],
        in_specs=[vmem] * 6,
        out_specs=[vmem] * 2,
        scratch_shapes=[pltpu.VMEM(here.shape, F32)],
        compiler_params=pltpu.CompilerParams(vmem_limit_bytes=SMALL_MIB * 2**20),
    )(here, there, densities.reshape(-1, gvectors), trial, energies, recycled)


def finish_kernel(product, recycled, arrived, image, coefficients):
    line = jnp.sum(arrived[...], 0, keepdims=True)
    count = recycled.shape[0]
    coefficients[...] = line[:, :count].reshape(count)
    at = lax.broadcasted_iota(jnp.int32, (count, 128), 0) == lax.broadcasted_iota(jnp.int32, (count, 128), 1)
    column = jnp.sum(jnp.where(at, jnp.broadcast_to(line, (count, 128)), 0.0), 1, keepdims=True)
    span = 512
    for g in range(product.shape[0] // span):
        taken = jnp.sum(recycled[:, g * span:(g + 1) * span] * column, 0, keepdims=True)
        at = pl.ds(g * span, span)
        image[at] = product[at] - taken.reshape(span)


def finish(product, recycled, arrived):
    vmem = pl.BlockSpec(memory_space=pltpu.VMEM)
    return pl.pallas_call(
        finish_kernel,
        out_shape=[jax.ShapeDtypeStruct(product.shape, F32), jax.ShapeDtypeStruct(recycled.shape[:1], F32)],
        in_specs=[vmem] * 3,
        out_specs=[vmem] * 2,
        compiler_params=pltpu.CompilerParams(vmem_limit_bytes=SMALL_MIB * 2**20),
    )(product, recycled, arrived)


def chip_groups(along_row, along_col):
    ids = np.arange(along_row * along_col * 2).reshape(along_row, along_col, 2)
    return [g.tolist() for g in ids[:, :, 0]] + [g.tolist() for g in ids[:, :, 1].T]


def body(trial, energies, densities, screening, pair_index, pair_count, recycled):
    kpoints, transitions, gvectors = densities.shape
    lanes = 128
    per_k = gvectors // lanes
    row_chips = lax.axis_size("zl") * lax.axis_size("x")
    col_chips = lax.axis_size("zh") * lax.axis_size("y")
    cores = lax.axis_size("c")
    col_devices = col_chips * cores
    row_place = lax.axis_index("zl") * lax.axis_size("x") + lax.axis_index("x")
    core = lax.axis_index("c")
    swap = [(0, 1), (1, 0)]
    groups = chip_groups(row_chips, col_chips)

    first_row = jnp.reshape(row_place * col_devices * kpoints, (1,)).astype(jnp.int32)
    local_dens = project(trial, densities)
    from_other = lax.ppermute(local_dens, "c", swap)
    place = core.reshape(1).astype(jnp.int32)
    out = jax.ShapeDtypeStruct((row_chips, 2 * local_dens.shape[0], lanes), BF16)
    index = jax.ShapeDtypeStruct(pair_index.shape[1:], jnp.int32)
    spread, rows, cols = local_call(
        functools.partial(pack_kernel, kpoints, col_devices * kpoints), [out, index, index],
        place, first_row, local_dens, from_other, pair_index, scalars=2)
    mine = lax.all_to_all(spread, AXES, 0, 0, axis_index_groups=groups).reshape(-1, lanes)
    theirs = lax.ppermute(mine, "c", swap)

    keep, send = pair_terms(rows, cols, pair_count, place, screening, mine, theirs)

    got = lax.ppermute(send, "c", swap)
    total = local_call(add_kernel, jax.ShapeDtypeStruct(keep.shape, BF16), keep, got)
    parts = lax.all_to_all(
        total.reshape(row_chips, -1, lanes), AXES, 0, 0, axis_index_groups=groups)
    part = (kpoints * per_k, lanes)
    away = (1 - core).reshape(1).astype(jnp.int32)
    there = local_call(sum_kernel, jax.ShapeDtypeStruct(part, BF16), away, parts, scalars=1)
    here = local_call(sum_kernel, jax.ShapeDtypeStruct(part, F32), place, parts, scalars=1)
    devices = row_chips * col_devices
    product, projections = expand(
        here, lax.ppermute(there, "c", swap), densities, trial, energies, recycled, devices)
    arrived = lax.all_to_all(projections, AXES, 0, 0, tiled=True)
    return tuple(finish(product, recycled, arrived))


def solution(mesh):
    fine = Mesh(mesh.devices.reshape(2, 4, 2, 4, 2), AXES)
    placed = (
        P(AXES),
        P(AXES),
        P(AXES, None, None),
        P(AXES, None),
        P(None, AXES),
        P(AXES),
        P(None, AXES),
    )
    return jax.shard_map(
        body, mesh=fine, in_specs=placed, out_specs=(P(AXES), P()), check_vma=False
    )
```

```python
import functools

import jax
import jax.numpy as jnp
import numpy as np
from jax import lax
from jax.experimental import pallas as pl
from jax.experimental.pallas import tpu as pltpu
from jax.sharding import Mesh, PartitionSpec as P

AXES = ("zl", "x", "zh", "y", "c")
F32 = jnp.float32
BF16 = jnp.bfloat16
COPIES = 4
SLOT_MIB = 48
SMALL_MIB = 6
DIAG_FLOPS = 4 * 10**9
STEP = 32
CHUNK = 2048
FIRST = 2048


def slot_kernel(row_index, col_index, count, place, weights, mine, theirs, keep, send,
                rows, cols, sem, part, part_sem, even, odd, rest, *tables):
    fetches = [pltpu.make_async_copy(row_index, rows, sem.at[0]),
               pltpu.make_async_copy(col_index, cols, sem.at[1])]
    for fetch in fetches:
        fetch.start()
    row_tables, col_tables = tables[:COPIES], tables[COPIES:]
    live, core = count[0], place[0]

    def part_copy(i):
        at = pl.ds(pl.multiple_of(i * CHUNK, CHUNK), CHUNK)
        return pltpu.make_async_copy(weights.at[at], part.at[at], part_sem.at[i])

    def part_start(i, _):
        part_copy(i).start()
        return 0

    lax.fori_loop(0, (live + CHUNK - 1) // CHUNK, part_start, 0)
    zeros = jnp.zeros((4, 128), F32)

    half = mine.shape[0] // 2
    block = half // (mine.shape[0] // 512)

    def fill(source, tables, count, dens_first, at):
        def step(i, _):
            part = source[pl.ds(pl.multiple_of(at(i), 16), 16), :].astype(F32)
            for t in range(4):
                dens = part[4 * t:4 * t + 4]
                entry = jnp.concatenate([dens, zeros] if dens_first else [zeros, dens], 0)
                for table in tables:
                    table[pl.ds(pl.multiple_of((i * 4 + t) * 8, 8), 8), :] = entry
            return 0

        lax.fori_loop(0, count // 16, step, 0, unroll=16)

    def whole(i):
        return i * 16

    def one_core(which):
        per = block // 16
        return lambda i: (i // per) * (2 * block) + which * block + (i % per) * 16

    @pl.when(core == 0)
    def _():
        fill(mine, row_tables, 2 * half, True, whole)
        fill(theirs, col_tables, half, False, one_core(0))

    @pl.when(core != 0)
    def _():
        fill(theirs, row_tables, 2 * half, True, whole)
        fill(mine, col_tables, half, False, one_core(1))

    low = lax.broadcasted_iota(jnp.int32, (8, 128), 0) >= 4

    def one(slot, which, row_weight, col_weight):
        r = pl.ds(pl.multiple_of(rows[slot], 8), 8)
        c = pl.ds(pl.multiple_of(cols[slot], 8), 8)
        row_entry = row_tables[which][r, :]
        col_entry = col_tables[which][c, :]
        row_tables[which][r, :] = row_entry + row_weight * col_entry
        col_tables[which][c, :] = col_entry + col_weight * row_entry

    def spread(first, target, at):
        for g in range(STEP // 16):
            v = part[pl.ds(pl.multiple_of(first + g * 16, 16), 16), :].astype(F32)
            for h in range(2):
                for j in range(4):
                    target[pl.ds(at + g * 64 + h * 32 + j * 8, 8), :] = v[8 * h:8 * h + 8, 128 * j:128 * j + 128]

    def many(first, source):
        for g in range(STEP // 16):
            for u in range(8):
                slot = first + g * 16 + u
                both = source[pl.ds(g * 64 + u, 8, stride=8), :]
                turned = jnp.concatenate([both[4:8], both[0:4]], 0)
                one(slot, (2 * u) % COPIES, jnp.where(low, turned, 0.0), jnp.where(low, 0.0, both))
                one(slot + 8, (2 * u + 1) % COPIES, jnp.where(low, both, 0.0), jnp.where(low, 0.0, turned))

    for fetch in fetches:
        fetch.wait()
    pairs = live // (2 * STEP)

    def pair(i, end):
        first = i * (2 * STEP)
        spread(first + STEP, odd, 0)
        many(first, even)
        spread(jnp.minimum(first + 2 * STEP, end * (2 * STEP) - STEP), even, 0)
        many(first + STEP, odd)
        return end

    def phase(n, _):
        begin = n * (FIRST // (2 * STEP))
        end = jnp.where(n == 0, jnp.minimum(pairs, FIRST // (2 * STEP)), pairs)

        def part_wait(i, _):
            part_copy(i).wait()
            return 0

        arrived = jnp.where(n == 0, jnp.minimum(live, FIRST), live)
        lax.fori_loop(n * (FIRST // CHUNK), (arrived + CHUNK - 1) // CHUNK, part_wait, 0)
        spread(begin * (2 * STEP), even, 0)
        lax.fori_loop(begin, end, pair, end)
        return 0

    lax.fori_loop(0, jnp.where(live > FIRST, 2, 1), phase, 0)
    done = pairs * (2 * STEP)
    @pl.when(live > done)
    def _():
        spread(done, rest, 0)
        spread(done + STEP, rest, 4 * STEP)

    def tail(slot, _):
        w = rest[pl.ds(slot // 8 * 32 + slot % 8, 4, stride=8), :]
        w = jnp.concatenate([w, w], 0)
        one(done + slot, 0, jnp.where(low, w, 0.0), jnp.where(low, 0.0, w))
        return 0

    lax.fori_loop(0, live - done, tail, 0)

    def drain(tables, target, count, at, offset):
        def step(i, _):
            parts = []
            for t in range(4):
                entry = pl.ds(pl.multiple_of((i * 4 + t) * 8, 8), 8)
                total = tables[0][entry, :]
                for table in tables[1:]:
                    total = total + table[entry, :]
                parts.append(total[offset:offset + 4])
            rows16 = pl.ds(pl.multiple_of(at(i), 16), 16)
            target[rows16, :] = jnp.concatenate(parts, 0).astype(BF16)
            return 0

        lax.fori_loop(0, count // 16, step, 0, unroll=16)

    def clear(target, at):
        def step(i, _):
            target[pl.ds(pl.multiple_of(at(i), 16), 16), :] = jnp.zeros((16, 128), BF16)
            return 0

        lax.fori_loop(0, half // 16, step, 0, unroll=8)

    @pl.when(core == 0)
    def _():
        drain(row_tables, keep, 2 * half, whole, 4)
        drain(col_tables, send, half, one_core(0), 0)
        clear(send, one_core(1))

    @pl.when(core != 0)
    def _():
        drain(row_tables, send, 2 * half, whole, 4)
        drain(col_tables, keep, half, one_core(1), 0)
        clear(keep, one_core(0))


def pair_terms(rows, cols, count, place, weights, mine, theirs):
    smem = pl.BlockSpec(memory_space=pltpu.SMEM)
    vmem = pl.BlockSpec(memory_space=pltpu.VMEM)
    hold = pl.BlockSpec(memory_space=pl.ANY)
    row_table = pltpu.VMEM((2 * mine.shape[0], 128), F32)
    col_table = pltpu.VMEM((mine.shape[0], 128), F32)
    return pl.pallas_call(
        slot_kernel,
        out_shape=[jax.ShapeDtypeStruct(mine.shape, BF16)] * 2,
        in_specs=[hold] * 2 + [smem] * 2 + [hold, vmem, vmem],
        out_specs=[vmem, vmem],
        scratch_shapes=[
            *[pltpu.SMEM(rows.shape, jnp.int32)] * 2, pltpu.SemaphoreType.DMA((2,)),
            pltpu.VMEM(weights.shape, BF16), pltpu.SemaphoreType.DMA((weights.shape[0] // CHUNK,)),
            *[pltpu.VMEM((STEP * 4, 128), F32)] * 2, pltpu.VMEM((STEP * 8, 128), F32),
            *[row_table] * COPIES, *[col_table] * COPIES],
        compiler_params=pltpu.CompilerParams(vmem_limit_bytes=SLOT_MIB * 2**20),
    )(rows, cols, count, place, weights, mine, theirs)


def local_call(kernel, outs, *args, scalars=0, flops=0):
    smem = pl.BlockSpec(memory_space=pltpu.SMEM)
    vmem = pl.BlockSpec(memory_space=pltpu.VMEM)
    return pl.pallas_call(
        kernel,
        out_shape=outs,
        in_specs=[smem] * scalars + [vmem] * (len(args) - scalars),
        out_specs=jax.tree.map(lambda _: vmem, outs),
        cost_estimate=pl.CostEstimate(flops=flops, bytes_accessed=0, transcendentals=0) if flops else None,
        compiler_params=pltpu.CompilerParams(vmem_limit_bytes=SMALL_MIB * 2**20),
    )(*args)


def pack_kernel(kpoints, spans, place, first_row, local, other, pair_index, out, rows, cols):
    index = pair_index[...]
    rows[...] = ((index[0:1, :] - first_row[0]) * 8).reshape(rows.shape)
    col = index[1:2, :]
    cols[...] = ((col // spans * kpoints + col % kpoints) * 8).reshape(cols.shape)
    size = local.shape[0]

    def step(i, _):
        at = pl.ds(pl.multiple_of(i * 16, 16), 16)
        first, second = local[at, :], other[at, :]
        swapped = place[0] != 0
        low = jnp.where(swapped, second.astype(F32), first.astype(F32)).astype(BF16)
        high = jnp.where(swapped, first.astype(F32), second.astype(F32)).astype(BF16)
        for n in range(out.shape[0]):
            out[n, at, :] = low
            out[n, pl.ds(pl.multiple_of(size + i * 16, 16), 16), :] = high
        return 0

    lax.fori_loop(0, size // 16, step, 0, unroll=2)


def add_kernel(keep, got, out):
    def step(i, _):
        at = pl.ds(pl.multiple_of(i * 16, 16), 16)
        out[at, :] = (keep[at, :].astype(F32) + got[at, :].astype(F32)).astype(BF16)
        return 0

    lax.fori_loop(0, keep.shape[0] // 16, step, 0, unroll=8)


def sum_kernel(other, place, parts, out):
    size = out.shape[0]
    which = 1 - place[0] if other else place[0]

    def step(i, _):
        first = pl.ds(pl.multiple_of(which * size + i * 16, 16), 16)
        total = parts[0, first, :].astype(F32)
        for n in range(1, parts.shape[0]):
            total = total + parts[n, first, :].astype(F32)
        out[pl.ds(pl.multiple_of(i * 16, 16), 16), :] = total.astype(out.dtype)
        return 0

    lax.fori_loop(0, size // 16, step, 0, unroll=4)


def diagonal_kernel(trial, out):
    span = out.shape[1]
    rows8 = lax.broadcasted_iota(jnp.int32, (8, span), 0)
    owner = lax.broadcasted_iota(jnp.int32, (8, span), 1) // (span // 8)
    for g in range(out.shape[0] // 16):
        both = []
        for n in (2 * g, 2 * g + 1):
            line = jnp.broadcast_to(trial[n * span:(n + 1) * span].reshape(1, span), (8, span))
            both.append(jnp.where(rows8 == owner, line, 0.0))
        out[16 * g:16 * g + 16, :] = jnp.concatenate(both, 0).astype(BF16)


def project_kernel(diagonal, densities, out, wide):
    kpoints, span = diagonal.shape
    for g in range(kpoints // 16):
        pair = diagonal[16 * g:16 * g + 16, :]
        for h in range(2):
            n = 2 * g + h
            dens = jnp.dot(pair[8 * h:8 * h + 8, :], densities[n * span:(n + 1) * span, :], preferred_element_type=F32)
            for j in range(4):
                wide[pl.ds(32 * n + j, 8, stride=4), :] = dens[:, 128 * j:128 * j + 128]
    out[...] = wide[...].astype(BF16)


def project(trial, densities):
    kpoints, transitions, gvectors = densities.shape
    vmem = pl.BlockSpec(memory_space=pltpu.VMEM)
    diagonal = local_call(
        diagonal_kernel, jax.ShapeDtypeStruct((kpoints, 8 * transitions), BF16), trial, flops=DIAG_FLOPS)
    return pl.pallas_call(
        project_kernel,
        out_shape=jax.ShapeDtypeStruct((kpoints * 4, 128), BF16),
        in_specs=[vmem, vmem],
        out_specs=vmem,
        scratch_shapes=[pltpu.VMEM((kpoints * 4, 128), F32)],
        cost_estimate=pl.CostEstimate(flops=4 * 10**9, bytes_accessed=0, transcendentals=0),
        compiler_params=pltpu.CompilerParams(vmem_limit_bytes=SMALL_MIB * 2**20),
    )(diagonal, densities.reshape(-1, gvectors))


def expand_kernel(here, there, densities, trial, energies, recycled, product, projections, field_sum):
    kpoints = here.shape[0] // 4
    span = densities.shape[0] * 8 // kpoints
    rows8 = lax.broadcasted_iota(jnp.int32, (8, span), 0)
    owner = lax.broadcasted_iota(jnp.int32, (8, span), 1) // (span // 8)
    sums = jnp.zeros((recycled.shape[0], 128), F32)
    field_sum[...] = here[...] + there[...].astype(F32)
    for g in range(kpoints // 8):
        field = []
        for j in range(4):
            at = pl.ds(32 * g + j, 8, stride=4)
            field.append(field_sum[at, :])
        every = lax.dot_general(
            jnp.concatenate(field, 1).astype(BF16), densities[g * span:(g + 1) * span, :],
            (((1,), (1,)), ((), ())), preferred_element_type=F32)
        part = jnp.sum(jnp.where(rows8 == owner, every, 0.0), 0, keepdims=True)
        at = pl.ds(g * span, span)
        line = (energies[at] * trial[at]).reshape(1, span) + part
        product[at] = line.reshape(span)
        weighted = recycled[:, g * span:(g + 1) * span] * line
        for j in range(span // 128):
            sums = sums + weighted[:, 128 * j:128 * j + 128]
    total = jnp.sum(sums, 1, keepdims=True)
    count = total.shape[0]
    at = lax.broadcasted_iota(jnp.int32, (count, 128), 0) == lax.broadcasted_iota(jnp.int32, (count, 128), 1)
    line = jnp.sum(jnp.where(at, total, 0.0), 0, keepdims=True)
    projections[...] = jnp.broadcast_to(line, projections.shape)


def expand(here, there, densities, trial, energies, recycled, devices):
    gvectors = densities.shape[-1]
    vmem = pl.BlockSpec(memory_space=pltpu.VMEM)
    return pl.pallas_call(
        expand_kernel,
        out_shape=[jax.ShapeDtypeStruct(trial.shape, F32), jax.ShapeDtypeStruct((devices, 128), F32)],
        in_specs=[vmem] * 6,
        out_specs=[vmem] * 2,
        scratch_shapes=[pltpu.VMEM(here.shape, F32)],
        compiler_params=pltpu.CompilerParams(vmem_limit_bytes=SMALL_MIB * 2**20),
    )(here, there, densities.reshape(-1, gvectors), trial, energies, recycled)


def finish_kernel(product, recycled, arrived, image, coefficients):
    line = jnp.sum(arrived[...], 0, keepdims=True)
    count = recycled.shape[0]
    coefficients[...] = line[:, :count].reshape(count)
    at = lax.broadcasted_iota(jnp.int32, (count, 128), 0) == lax.broadcasted_iota(jnp.int32, (count, 128), 1)
    column = jnp.sum(jnp.where(at, jnp.broadcast_to(line, (count, 128)), 0.0), 1, keepdims=True)
    span = 512
    for g in range(product.shape[0] // span):
        taken = jnp.sum(recycled[:, g * span:(g + 1) * span] * column, 0, keepdims=True)
        at = pl.ds(g * span, span)
        image[at] = product[at] - taken.reshape(span)


def finish(product, recycled, arrived):
    vmem = pl.BlockSpec(memory_space=pltpu.VMEM)
    return pl.pallas_call(
        finish_kernel,
        out_shape=[jax.ShapeDtypeStruct(product.shape, F32), jax.ShapeDtypeStruct(recycled.shape[:1], F32)],
        in_specs=[vmem] * 3,
        out_specs=[vmem] * 2,
        compiler_params=pltpu.CompilerParams(vmem_limit_bytes=SMALL_MIB * 2**20),
    )(product, recycled, arrived)


def chip_groups(along_row, along_col):
    ids = np.arange(along_row * along_col * 2).reshape(along_row, along_col, 2)
    return [g.tolist() for g in ids[:, :, 0]] + [g.tolist() for g in ids[:, :, 1].T]


def body(trial, energies, densities, screening, pair_index, pair_count, recycled):
    kpoints, transitions, gvectors = densities.shape
    lanes = 128
    per_k = gvectors // lanes
    row_chips = lax.axis_size("zl") * lax.axis_size("x")
    col_chips = lax.axis_size("zh") * lax.axis_size("y")
    cores = lax.axis_size("c")
    col_devices = col_chips * cores
    row_place = lax.axis_index("zl") * lax.axis_size("x") + lax.axis_index("x")
    core = lax.axis_index("c")
    swap = [(0, 1), (1, 0)]
    groups = chip_groups(row_chips, col_chips)

    first_row = jnp.reshape(row_place * col_devices * kpoints, (1,)).astype(jnp.int32)
    local_dens = project(trial, densities)
    from_other = lax.ppermute(local_dens, "c", swap)
    place = core.reshape(1).astype(jnp.int32)
    out = jax.ShapeDtypeStruct((row_chips, 2 * local_dens.shape[0], lanes), BF16)
    index = jax.ShapeDtypeStruct(pair_index.shape[1:], jnp.int32)
    spread, rows, cols = local_call(
        functools.partial(pack_kernel, kpoints, col_devices * kpoints), [out, index, index],
        place, first_row, local_dens, from_other, pair_index, scalars=2)
    mine = lax.all_to_all(spread, AXES, 0, 0, axis_index_groups=groups).reshape(-1, lanes)
    theirs = lax.ppermute(mine, "c", swap)

    keep, send = pair_terms(rows, cols, pair_count, place, screening, mine, theirs)

    got = lax.ppermute(send, "c", swap)
    total = local_call(add_kernel, jax.ShapeDtypeStruct(keep.shape, BF16), keep, got)
    parts = lax.all_to_all(
        total.reshape(row_chips, -1, lanes), AXES, 0, 0, axis_index_groups=groups)
    part = (kpoints * per_k, lanes)
    there = local_call(
        functools.partial(sum_kernel, True), jax.ShapeDtypeStruct(part, BF16), place, parts, scalars=1)
    here = local_call(
        functools.partial(sum_kernel, False), jax.ShapeDtypeStruct(part, F32), place, parts, scalars=1)
    devices = row_chips * col_devices
    product, projections = expand(
        here, lax.ppermute(there, "c", swap), densities, trial, energies, recycled, devices)
    arrived = lax.all_to_all(projections, AXES, 0, 0, tiled=True)
    return tuple(finish(product, recycled, arrived))


def solution(mesh):
    fine = Mesh(mesh.devices.reshape(2, 4, 2, 4, 2), AXES)
    placed = (
        P(AXES),
        P(AXES),
        P(AXES, None, None),
        P(AXES, None),
        P(None, AXES),
        P(AXES),
        P(None, AXES),
    )
    return jax.shard_map(
        body, mesh=fine, in_specs=placed, out_specs=(P(AXES), P()), check_vma=False
    )
```
